512 devices in a mesh: replica: 32 (over y_lo, z, core), tensor: 16 (over y_hi, x).
Axes of the slice: x: 4, y: 8 (y_hi: 4, y_lo: 2; y = y_hi * 2 + y_lo), z: 8, core: 2. Of those that a mesh axis runs over, the one named last changes fastest.
Arguments:
- span_query: bfloat16 [8192, 8192], P('replica', 'tensor'), may hold values from -16 to 16
- span_kv: bfloat16 [8192, 4096], P('replica', 'tensor'), may hold values from -6 to 6, as said below
- kv_pool: bfloat16 [512, 128, 4096], P('replica', None, 'tensor'), may hold values from -8 to 8, as said below
- hit_owner: int32 [1024, 1], P('replica'), may hold values from 0 to 31; in each aligned block of 32 rows (0 to 31, 32 to 63, ...) at most 2 rows name the same one
- hit_slot: int32 [1024], P('replica'), may hold values from 0 to 15
- decode_query: bfloat16 [1024, 8192], P('replica', 'tensor'), may hold values from -16 to 16
- decode_kv: bfloat16 [1024, 4096], P('replica', 'tensor'), may hold values from -6 to 6, as said below
- decode_table: int32 [1024, 4], P('replica'), may hold values from 0 to 15
- decode_length: int32 [32, 32], P('replica'), may hold values from 1 to 512, 8192 in all within a row
Outputs:
- span_out: bfloat16 [8192, 8192], P('replica', 'tensor')
- decode_out: bfloat16 [1024, 8192], P('replica', 'tensor')
The draws below stay inside these ranges and needn't reach their ends.
Inputs may be any that keep to these rules, and one draw needn't show every extreme that they name: `hit_owner`: among the 32 hits of one replica, at most 2 name the same owner. `kv_pool`: the 2 copies of a head are equal. `span_kv`: the 2 copies of a head are equal. `decode_kv`: the 2 copies of a head are equal.
All inputs are finite; a program needn't handle non-finite values.
Results may differ from the reference program's by a relative error of at most 0.009.
Values may be sent and summed in bfloat16 or wider, within the bound.
A program may use at most 64 MiB of HBM per device.

```python
import math
import jax
import jax.numpy as jnp
import numpy as np
from jax import lax

QH = 64
KVH = 8
HD = 128
BLK = 128
SPAN = 256
PB = 32
POOL = 16
DEC = 32
MAXB = 4
CAP = 2
REP = 2
QW = 8192
KVW = 2048
SPAN_ROWS = 8192
DEC_ROWS = 1024
HITS = 1024
SLOTS = 512
N_REPLICA = 32


def copy_heads(base):
    lead = base.shape[:-3]
    widened = jnp.broadcast_to(base[..., None, :, :], lead + (KVH, REP, 2, HD))
    return widened.reshape(lead + (REP * KVW,))


def draw_span_query(key, part):
    key = jax.random.fold_in(key, 11)
    return jnp.clip(jax.random.normal(key, (SPAN_ROWS, QW), jnp.float32), -6.0, 6.0).astype(jnp.bfloat16)


def draw_decode_query(key, part):
    key = jax.random.fold_in(key, 12)
    return jnp.clip(jax.random.normal(key, (DEC_ROWS, QW), jnp.float32), -6.0, 6.0).astype(jnp.bfloat16)


def draw_span_kv(key, part):
    key = jax.random.fold_in(key, 14)
    base = jnp.clip(jax.random.normal(key, (SPAN_ROWS, KVH, 2, HD), jnp.float32), -6.0, 6.0)
    return copy_heads(base).astype(jnp.bfloat16)


def draw_decode_kv(key, part):
    key = jax.random.fold_in(key, 15)
    base = jnp.clip(jax.random.normal(key, (DEC_ROWS, KVH, 2, HD), jnp.float32), -6.0, 6.0)
    return copy_heads(base).astype(jnp.bfloat16)


def draw_kv_pool(key, part):
    key = jax.random.fold_in(key, 13)
    base = jnp.clip(jax.random.normal(key, (SLOTS, BLK, KVH, 2, HD), jnp.float32), -6.0, 6.0)
    return copy_heads(base).astype(jnp.bfloat16)


def set_ends(drawn, stream_key, low, high):
    extent = drawn.shape
    index_at = [jax.random.randint(jax.random.fold_in(stream_key, axis), (), 0, extent[axis]) for axis in range(len(extent))]
    drawn = drawn.at[tuple(index_at)].set(low)
    longest = extent.index(max(extent))
    index_at[longest] = (index_at[longest] + 1) % extent[longest]
    return drawn.at[tuple(index_at)].set(high)


def length_profile(amount, total, bound, lean):
    weights = [(1 << 20) // math.isqrt(standing ** lean) + 1 for standing in range(2, amount + 1)]
    spare, given = total - bound - (amount - 1), [1] * (amount - 1)
    while spare > 0:
        movable = [i for i in range(amount - 1) if given[i] < bound]
        mass, budget = sum([weights[i] for i in movable]), spare
        for i in movable:
            extra = min(bound - given[i], max(1, budget * weights[i] // mass), spare)
            given[i] = given[i] + extra
            spare = spare - extra
    return np.array([bound] + given)


def ragged_sizes(stream_key, count, total, most, skew):
    if count == 2:
        one = jax.random.randint(stream_key, (), max(1, total - most), min(most, total - 1) + 1)
        return jnp.stack([one, total - one])
    tallies = jnp.asarray(length_profile(count, total, most, skew), jnp.int32)
    pairs = (count - 1) // 2
    source_of, sink = tallies[1:1 + 2 * pairs:2], tallies[2:2 + 2 * pairs:2]
    slack = jnp.minimum(source_of - 1, most - sink)
    moved = jax.random.randint(jax.random.fold_in(stream_key, 1), (pairs,), 0, 1 << 20) % (slack + 1)
    tallies = tallies.at[1:1 + 2 * pairs:2].set(source_of - moved).at[2:2 + 2 * pairs:2].set(sink + moved)
    return tallies[jax.random.permutation(jax.random.fold_in(stream_key, 2), count)]


def shared_out(rng, own, number, rows, amount, top, bound, skew):
    sequence = jax.random.permutation(rng, amount)
    packed, usual = load_shares(amount, rows * top, bound, skew, True), load_shares(amount, rows * top, bound, skew, False)
    places = jnp.arange(amount)

    def named(sizes, rotation):
        used = int((sizes > 0).sum())
        fixed = max(1, used // 4)
        passed = fixed + (places - fixed + rotation * (used - fixed)) % max(1, amount - fixed)
        return jnp.zeros((amount,), jnp.int32).at[sequence[jnp.where(places < fixed, places, passed)]].set(jnp.asarray(sizes, jnp.int32))

    sizes = jnp.where(number % 4 == 0, named(packed, number // 4), named(usual, number - number // 4 - 1))
    mixed = jax.random.permutation(jax.random.fold_in(own, 3), amount)
    giver, sink = mixed[0:amount // 2 * 2:2], mixed[1:amount // 2 * 2:2]
    margin = jnp.minimum(sizes[giver] - 1, bound - sizes[sink]) // 2
    margin = jnp.where((giver == sequence[0]) | (sink == sequence[0]) | (sizes[sink] == 0), 0, jnp.maximum(margin, 0))
    passed = jax.random.randint(jax.random.fold_in(own, 4), (amount // 2,), 0, 1 << 20) % (margin + 1)
    sizes = sizes.at[giver].add(-passed).at[sink].add(passed)
    members = jnp.searchsorted(jnp.cumsum(sizes), jnp.arange(rows * top), side="right").astype(jnp.int32)
    listing = members.reshape(top, rows).T
    listing = listing[jax.random.permutation(jax.random.fold_in(own, 1), rows)]
    rotation = jax.random.randint(jax.random.fold_in(own, 2), (rows, 1), 0, top)
    return jnp.take_along_axis(listing, (jnp.arange(top)[None, :] + rotation) % top, axis=1)


def load_shares(amount, total, most, slope, full):
    weights = [(1 << 20) // math.isqrt(standing ** slope) + 1 for standing in range(1, amount + 1)]
    largest = most if full else min(most, max(-(-total // amount), total * weights[0] // sum(weights)))
    least = 1 if total - largest >= amount - 1 else 0
    holding, surplus = [largest] + [least] * (amount - 1), total - largest - least * (amount - 1)
    while surplus > 0:
        candidates = [i for i in range(1, amount) if holding[i] < largest] or [i for i in range(1, amount) if holding[i] < most]
        mass, left = sum([weights[i] for i in candidates]), surplus
        for i in candidates:
            extra = min(most - holding[i], max(1, left * weights[i] // mass), surplus)
            holding[i] = holding[i] + extra
            surplus = surplus - extra
    return np.array(holding)


def setup_inputs(seed: int = 0) -> dict:
    splits = jax.random.split(jax.random.key(seed), 10)
    span_query = draw_span_query(jax.random.fold_in(splits[9], 71), 0)
    span_kv = draw_span_kv(jax.random.fold_in(splits[9], 71), 0)
    kv_pool = draw_kv_pool(jax.random.fold_in(splits[9], 71), 0)
    hit_owner_keys = jax.random.split(jax.random.fold_in(splits[3], 1), HITS // PB)
    hit_owner_turns = jax.random.permutation(jax.random.fold_in(splits[3], 3), HITS // PB)
    hit_owner = jax.vmap(lambda own, number: shared_out(jax.random.fold_in(splits[3], 2), own, number, PB, N_REPLICA, 1, CAP, 2))(hit_owner_keys, hit_owner_turns).reshape((HITS, 1))
    hit_slot = set_ends(jax.random.randint(splits[4], (HITS,), 0, POOL), jax.random.fold_in(splits[4], 1), 0, POOL - 1).astype(jnp.int32)
    decode_query = draw_decode_query(jax.random.fold_in(splits[9], 71), 0)
    decode_kv = draw_decode_kv(jax.random.fold_in(splits[9], 71), 0)
    decode_table = set_ends(jax.random.randint(splits[7], (DEC_ROWS, MAXB), 0, POOL), jax.random.fold_in(splits[7], 1), 0, POOL - 1).astype(jnp.int32)
    decode_length = jax.vmap(lambda own: ragged_sizes(own, DEC, DEC * MAXB * BLK // 2, MAXB * BLK, 2))(jax.random.split(splits[8], N_REPLICA)).reshape((N_REPLICA, DEC)).astype(jnp.int32)
    return {"span_query": span_query, "span_kv": span_kv, "kv_pool": kv_pool, "hit_owner": hit_owner, "hit_slot": hit_slot, "decode_query": decode_query, "decode_kv": decode_kv, "decode_table": decode_table, "decode_length": decode_length}


def soft_mix(scores, allowed, values):
    masked = jnp.where(allowed, scores, -1e30)
    highest = jnp.max(masked, axis=-1, keepdims=True)
    weights = jnp.where(allowed, jnp.exp(masked - highest), 0.0)
    weight_sum = jnp.sum(weights, axis=-1, keepdims=True)
    rounded = lax.optimization_barrier(weights.astype(jnp.bfloat16)).astype(jnp.float32)
    mixture = jnp.einsum("grl,lh->grh", rounded, values.astype(jnp.float32))
    return mixture / weight_sum


def reference(span_query, span_kv, kv_pool, hit_owner, hit_slot, decode_query, decode_kv, decode_table, decode_length):
    inv_root = HD ** -0.5
    group = QH // KVH
    blocks = kv_pool.reshape(SLOTS, BLK, KVH, REP, 2, HD)[:, :, :, 0]
    owners = hit_owner.reshape(N_REPLICA, PB)
    slots = hit_slot.reshape(N_REPLICA, PB)
    queries = span_query.reshape(N_REPLICA, SPAN, KVH, group, HD)
    fresh = span_kv.reshape(N_REPLICA, SPAN, KVH, REP, 2, HD)[:, :, :, 0]
    causal = jnp.arange(SPAN)[:, None] >= jnp.arange(SPAN)[None, :]
    allowed = jnp.concatenate([causal, jnp.ones((SPAN, PB * BLK), dtype=bool)], axis=1)

    def prefill(inputs):
        query_rows, fresh_rows, owner_rows, slot_rows = inputs
        picks = (owner_rows * POOL + slot_rows).astype(jnp.int32)
        fetched = blocks[picks].reshape(PB * BLK, KVH, 2, HD)
        context = jnp.concatenate([fresh_rows, fetched], axis=0)

        def per_head(head_inputs):
            head_query, head_context = head_inputs
            scores = jnp.einsum("rgh,lh->grl", head_query.astype(jnp.float32), head_context[:, 0].astype(jnp.float32)) * inv_root
            return soft_mix(scores, allowed[None], head_context[:, 1])

        mixture = lax.map(per_head, (jnp.moveaxis(query_rows, 1, 0), jnp.moveaxis(context, 1, 0)))
        return jnp.transpose(mixture, (2, 0, 1, 3)).reshape(SPAN, QW).astype(jnp.bfloat16)

    span_out = lax.map(prefill, (queries, fresh, owners, slots)).reshape(SPAN_ROWS, QW)

    dec_queries = decode_query.reshape(N_REPLICA, DEC, KVH, group, HD)
    own_pairs = decode_kv.reshape(N_REPLICA, DEC, KVH, REP, 2, HD)[:, :, :, 0]
    tables = decode_table.reshape(N_REPLICA, DEC, MAXB)
    positions = jnp.arange(MAXB * BLK)

    def decode(inputs):
        query_rows, own_rows, table_rows, length_rows, replica = inputs
        picks = (replica * POOL + table_rows).astype(jnp.int32)
        cache = blocks[picks].reshape(DEC, MAXB * BLK, KVH, 2, HD)
        query_wide = query_rows.astype(jnp.float32)
        scores = jnp.einsum("dkgh,dtkh->dkgt", query_wide, cache[:, :, :, 0].astype(jnp.float32)) * inv_root
        own_score = jnp.einsum("dkgh,dkh->dkg", query_wide, own_rows[:, :, 0].astype(jnp.float32)) * inv_root
        usable = (positions[None, :] < length_rows[:, None])[:, None, None, :]
        masked = jnp.where(usable, scores, -1e30)
        highest = jnp.maximum(jnp.max(masked, axis=-1), own_score)
        weights = jnp.where(usable, jnp.exp(masked - highest[..., None]), 0.0)
        own_weight = jnp.exp(own_score - highest)
        weight_sum = jnp.sum(weights, axis=-1) + own_weight
        rounded = lax.optimization_barrier(weights.astype(jnp.bfloat16)).astype(jnp.float32)
        own_rounded = lax.optimization_barrier(own_weight.astype(jnp.bfloat16)).astype(jnp.float32)
        mixture = jnp.einsum("dkgt,dtkh->dkgh", rounded, cache[:, :, :, 1].astype(jnp.float32))
        mixture = mixture + own_rounded[..., None] * own_rows[:, :, 1].astype(jnp.float32)[:, :, None, :]
        return (mixture / weight_sum[..., None]).reshape(DEC, QW).astype(jnp.bfloat16)

    replica_ids = jnp.arange(N_REPLICA).astype(jnp.int32)
    decode_out = lax.map(decode, (dec_queries, own_pairs, tables, decode_length, replica_ids)).reshape(DEC_ROWS, QW)
    return span_out, decode_out
```

```python
import functools
import math

import jax
import jax.numpy as jnp
from jax import lax
from jax.experimental import pallas as pl
from jax.experimental.pallas import tpu as pltpu
from jax.sharding import PartitionSpec as P

MESH = pl.DeviceIdType.MESH
HD = 128
NZ = 8
HALF = 64
CHUNKS = 4
SCALE = HD ** (-0.5) * math.log2(math.e)
LOW = -1e30


def nt_dot(a, b):
    return lax.dot_general(a, b, (((1,), (1,)), ((), ())), preferred_element_type=jnp.float32)


def column(row):
    n = row.shape[1]
    eye = lax.broadcasted_iota(jnp.int32, (n, n), 0) == lax.broadcasted_iota(jnp.int32, (n, n), 1)
    return jnp.sum(jnp.where(eye, jnp.broadcast_to(row, (n, n)), 0.0), axis=1, keepdims=True)


def as_row(replicated):
    eye = lax.broadcasted_iota(jnp.int32, (128, 128), 0) == lax.broadcasted_iota(
        jnp.int32, (128, 128), 1
    )
    return jnp.sum(jnp.where(eye, replicated, 0.0), axis=0, keepdims=True)


def kernel(
    owner_s,
    slot_s,
    table_ref,
    length_ref,
    dq_ref,
    dkv_ref,
    skv_ref,
    q_hbm,
    pool_hbm,
    span_out,
    decode_out,
    pool_v,
    qall,
    up1,
    up2,
    up3,
    down1,
    down2,
    down3,
    far,
    stage,
    inbox,
    tabs,
    tabs_s,
    acc,
    top,
    total,
    part_out,
    part_in,
    stat_out,
    stat_in,
    load_sem,
    zsend,
    zrecv,
    psend,
    precv,
    tsend,
    trecv,
    smem_sem,
    qsend,
    qrecv,
    osend,
    orecv,
    ssend,
    srecv,
):
    r = lax.axis_index("replica")
    t = lax.axis_index("tensor")
    yl, z, c = r // 16, (r // 2) % NZ, r % 2
    xh = t % 2
    tx = t + 1 - 2 * xh

    def at_z(step):
        return (yl * 16 + ((z + step + NZ) % NZ) * 2 + c, t)

    def peer(e):
        py = yl if e < 2 else 1 - yl
        pc = c if e % 2 == 0 else 1 - c
        return (py, pc)

    def peer_id(e):
        py, pc = peer(e)
        return (py * 16 + z * 2 + pc, t)

    xid = (r, tx)
    buf = ((up1, up2, up3, far), (down1, down2, down3, far))
    ahead = (at_z(1), at_z(-1))

    barrier = pltpu.get_barrier_semaphore()
    for other in ahead + (peer_id(1), peer_id(2), peer_id(3), xid):
        pl.semaphore_signal(barrier, inc=1, device_id=other, device_id_type=MESH)

    loads = [pltpu.make_async_copy(pool_hbm, pool_v, load_sem.at[0])]
    for h in range(4):
        loads.append(
            pltpu.make_async_copy(
                q_hbm.at[:, pl.ds(h * HD, HD)], qall.at[h], load_sem.at[1 + h]
            )
        )
    for copy in loads:
        copy.start()

    pl.semaphore_wait(barrier, 6)

    per = 16 // CHUNKS

    def ring(d, k, ch):
        rows = pl.ds(ch * per, per)
        if k == 1:
            src = pool_hbm.at[rows, pl.ds(pl.multiple_of(xh * HALF, HALF), HALF), :]
        else:
            src = buf[d][k - 2].at[rows]
        return pltpu.make_async_remote_copy(
            src_ref=src,
            dst_ref=buf[d][k - 1].at[rows],
            send_sem=zsend.at[d, k - 1, ch],
            recv_sem=zrecv.at[d, k - 1, ch],
            device_id=ahead[d],
            device_id_type=MESH,
        )

    def chunks_of(d, k):
        if k < 4:
            return range(CHUNKS)
        return range(CHUNKS // 2) if d == 0 else range(CHUNKS // 2, CHUNKS)

    for ch in range(CHUNKS):
        for d in range(2):
            ring(d, 1, ch).start()

    def query_copy(h):
        return pltpu.make_async_remote_copy(
            src_ref=q_hbm.at[:, pl.ds(h * HD, HD)],
            dst_ref=qall.at[4 + h],
            send_sem=qsend.at[h],
            recv_sem=qrecv.at[h],
            device_id=xid,
            device_id_type=MESH,
        )

    for h in range(4):
        query_copy(h).start()

    lane = lax.broadcasted_iota(jnp.int32, (8, 128), 1)
    lane_owner, lane_rank = lane // 2, lane % 2

    def note_hit(i, carried):
        table, seen = carried
        match = lane_owner == owner_s[i]
        table = jnp.where(match & (seen == lane_rank), slot_s[i], table)
        return table, seen + match.astype(jnp.int32)

    table, _ = lax.fori_loop(
        0,
        32,
        note_hit,
        (jnp.full((8, 128), -1, jnp.int32), jnp.zeros((8, 128), jnp.int32)),
    )
    tabs[0] = table

    def table_copy(e):
        return pltpu.make_async_remote_copy(
            src_ref=tabs.at[0],
            dst_ref=tabs.at[e],
            send_sem=tsend.at[e],
            recv_sem=trecv.at[e],
            device_id=peer_id(e),
            device_id_type=MESH,
        )

    for e in range(1, 4):
        table_copy(e).start()

    loads[0].wait()
    for e in range(4):
        if e:
            table_copy(e).wait_recv()
        moved = pltpu.make_async_copy(tabs.at[e], tabs_s.at[e], smem_sem.at[e])
        moved.start()
        moved.wait()

    def plane_z(p):
        step = -p if p < 5 else p - 4
        return (z + step + NZ) % NZ

    def hand_copy(p, e):
        return pltpu.make_async_remote_copy(
            src_ref=stage.at[p, e],
            dst_ref=inbox.at[p, e],
            send_sem=psend.at[p, e],
            recv_sem=precv.at[p, e],
            device_id=peer_id(e),
            device_id_type=MESH,
        )

    def hand_out(p):
        owner = yl * 16 + plane_z(p) * 2 + c
        for e in (3, 2, 1, 0):
            for rank in range(2):
                slot = jnp.clip(tabs_s[e, 0, owner * 2 + rank], 0, 15)
                if p == 0:
                    rows = pool_v[slot, pl.ds(pl.multiple_of(xh * HALF, HALF), HALF), :]
                elif p < 5:
                    rows = buf[0][p - 1][slot]
                else:
                    rows = buf[1][p - 5][slot]
                place = pl.ds(rank * HALF, HALF)
                if e == 0:
                    inbox[p, 0, place, :] = rows
                else:
                    stage[p, e, place, :] = rows
            if e:
                hand_copy(p, e).start()

    hand_out(0)

    count = 32
    dq = jnp.concatenate([dq_ref[:, pl.ds(g * HD, HD)] for g in range(4)], axis=0)
    lengths = column(length_ref[...].astype(jnp.float32))
    names = [column(table_ref[b : b + 1, :].astype(jnp.float32)) for b in range(4)]
    spot = lax.broadcasted_iota(jnp.int32, (count, HD), 1).astype(jnp.float32)

    def times(block):
        name = jnp.float32(1) * block
        seen = jnp.zeros((count, HD), jnp.float32)
        for b in range(4):
            limit = jnp.where(names[b] == name, lengths - 128.0 * b, 0.0)
            seen = seen + jnp.where(spot < limit, 1.0, 0.0)
        return jnp.concatenate([seen] * 4, axis=0)

    own_key = jnp.concatenate([dkv_ref[:, :HD].astype(jnp.float32)] * 4, axis=0)
    own_value = jnp.concatenate([dkv_ref[:, HD:].astype(jnp.float32)] * 4, axis=0)
    own_score = jnp.sum(dq.astype(jnp.float32) * own_key, axis=1, keepdims=True)

    def decode_step(it, carried):
        highest, weight_sum, mixture = carried
        rows = pool_v[pl.ds(it * 4, 4)].reshape(4 * HD, 2 * HD)
        scores = nt_dot(dq, rows[:, :HD])
        seen = jnp.concatenate([times((it * 4 + i).astype(jnp.float32)) for i in range(4)], axis=1)
        masked = jnp.where(seen > 0.0, scores, LOW)
        raised = jnp.maximum(highest, jnp.max(masked, axis=1, keepdims=True))
        weights = jnp.exp2((masked - raised) * SCALE)
        shrink = jnp.exp2((highest - raised) * SCALE)
        weight_sum = weight_sum * shrink + jnp.sum(weights * seen, axis=1, keepdims=True)
        spread = (weights.astype(jnp.bfloat16).astype(jnp.float32) * seen).astype(jnp.bfloat16)
        mixture = mixture * shrink + jnp.dot(
            spread, rows[:, HD:], preferred_element_type=jnp.float32
        )
        return raised, weight_sum, mixture

    _, weight_sum, mixture = lax.fori_loop(
        0, 4, decode_step, (own_score, jnp.ones((128, 1), jnp.float32), own_value)
    )
    mixed = (mixture / weight_sum).astype(jnp.bfloat16)
    for g in range(4):
        decode_out[:, pl.ds(g * HD, HD)] = mixed[g * count : (g + 1) * count]

    for copy in loads[1:]:
        copy.wait()
    fresh_keys, fresh_values = skv_ref[:, :HD], skv_ref[:, HD:]
    causal = lax.broadcasted_iota(jnp.int32, (256, 256), 0) >= lax.broadcasted_iota(
        jnp.int32, (256, 256), 1
    )

    def fresh_step(h, carried):
        masked = jnp.where(causal, nt_dot(qall[h], fresh_keys), LOW)
        highest = jnp.max(masked, axis=1, keepdims=True)
        weights = jnp.exp2((masked - highest) * SCALE)
        top[h] = jnp.broadcast_to(highest, (256, HD))
        total[h] = weights[:, :HD] + weights[:, HD:]
        acc[h] = jnp.dot(
            weights.astype(jnp.bfloat16), fresh_values, preferred_element_type=jnp.float32
        )
        top[4 + h] = jnp.full((256, HD), LOW, jnp.float32)
        total[4 + h] = jnp.zeros((256, HD), jnp.float32)
        acc[4 + h] = jnp.zeros((256, HD), jnp.float32)
        return carried

    lax.fori_loop(0, 4, fresh_step, 0)
    for h in range(4):
        query_copy(h).wait_recv()

    cell = lax.broadcasted_iota(jnp.int32, (1, 512), 1) // HALF

    def attend(p, first, count):
        bias = jnp.zeros((1, 512), jnp.float32)
        for e in range(4):
            py, pc = peer(e)
            owner = py * 16 + plane_z(p) * 2 + pc
            for rank in range(2):
                asked = tabs_s[0, 0, owner * 2 + rank]
                bias = jnp.where(
                    (cell == 2 * e + rank) & (jnp.full((1, 512), asked, jnp.int32) < 0), LOW, bias
                )

        def fold(h, carried):
            rows = inbox[p].reshape(512, 2 * HD)
            scores = nt_dot(qall[h], rows[:, :HD]) + bias
            highest = top[h][:, :1]
            raised = jnp.maximum(highest, jnp.max(scores, axis=1, keepdims=True))
            weights = jnp.exp2((scores - raised) * SCALE)
            shrink = jnp.exp2((highest - raised) * SCALE)
            top[h] = jnp.broadcast_to(raised, (256, HD))
            total[h] = total[h] * shrink + (
                (weights[:, :HD] + weights[:, HD : 2 * HD])
                + (weights[:, 2 * HD : 3 * HD] + weights[:, 3 * HD :])
            )
            acc[h] = acc[h] * shrink + jnp.dot(
                weights.astype(jnp.bfloat16), rows[:, HD:], preferred_element_type=jnp.float32
            )
            return carried

        lax.fori_loop(first, first + count, fold, 0)

    def collect(p):
        for e in range(1, 4):
            hand_copy(p, e).wait_recv()

    planes = ((0,), (1, 5), (2, 6), (3, 7), (4,))
    for k in range(1, 5):
        for i in range(CHUNKS):
            for d in range(2):
                if i < len(chunks_of(d, k)):
                    ch = chunks_of(d, k)[i]
                    ring(d, k, ch).wait_recv()
                    if k < 4 and ch in chunks_of(d, k + 1):
                        ring(d, k + 1, ch).start()
        for p in planes[k]:
            hand_out(p)
        for p in planes[k - 1]:
            collect(p)
            attend(p, 0, 8)

    def part_copy(h):
        return pltpu.make_async_remote_copy(
            src_ref=part_out.at[h],
            dst_ref=part_in.at[h],
            send_sem=osend.at[h],
            recv_sem=orecv.at[h],
            device_id=xid,
            device_id_type=MESH,
        )

    def stat_copy(h):
        return pltpu.make_async_remote_copy(
            src_ref=stat_out.at[h],
            dst_ref=stat_in.at[h],
            send_sem=ssend.at[h],
            recv_sem=srecv.at[h],
            device_id=xid,
            device_id_type=MESH,
        )

    collect(4)
    attend(4, 4, 4)
    for h in range(4):
        part_out[h] = acc[4 + h].astype(jnp.bfloat16)
        stat_out[h] = jnp.zeros((8, HD), jnp.float32)
        for i in range(2):
            rows = pl.ds(i * HD, HD)
            sums = jnp.sum(total[4 + h, rows, :], axis=1, keepdims=True)
            stat_out[h, i : i + 1, :] = as_row(top[4 + h, rows, :])
            stat_out[h, 2 + i : 3 + i, :] = as_row(jnp.broadcast_to(sums, (HD, HD)))
        part_copy(h).start()
        stat_copy(h).start()
    attend(4, 0, 4)
    for h in range(4):
        part_copy(h).wait_recv()
        stat_copy(h).wait_recv()
        for i in range(2):
            rows = pl.ds(i * HD, HD)
            here, there = top[h, rows, :][:, :1], column(stat_in[h, i : i + 1, :])
            peak = jnp.maximum(here, there)
            keep, take = jnp.exp2((here - peak) * SCALE), jnp.exp2((there - peak) * SCALE)
            sums = (
                jnp.sum(total[h, rows, :], axis=1, keepdims=True) * keep
                + column(stat_in[h, 2 + i : 3 + i, :]) * take
            )
            mixed = acc[h, rows, :] * keep + part_in[h, rows, :].astype(jnp.float32) * take
            span_out[rows, pl.ds(h * HD, HD)] = (mixed / sums).astype(jnp.bfloat16)

    for k in range(1, 5):
        for d in range(2):
            for ch in chunks_of(d, k):
                ring(d, k, ch).wait_send()
    for h in range(4):
        query_copy(h).wait_send()
        part_copy(h).wait_send()
        stat_copy(h).wait_send()
    for e in range(1, 4):
        table_copy(e).wait_send()
        for p in range(NZ):
            hand_copy(p, e).wait_send()


def local(
    span_query,
    span_kv,
    kv_pool,
    hit_owner,
    hit_slot,
    decode_query,
    decode_kv,
    decode_table,
    decode_length,
):
    vmem = pl.BlockSpec(memory_space=pltpu.VMEM)
    smem = pl.BlockSpec(memory_space=pltpu.SMEM)
    hbm = pl.BlockSpec(memory_space=pl.ANY)
    dma = pltpu.SemaphoreType.DMA
    bf16, f32 = jnp.bfloat16, jnp.float32
    return pl.pallas_call(
        kernel,
        out_shape=(
            jax.ShapeDtypeStruct(span_query.shape, bf16),
            jax.ShapeDtypeStruct(decode_query.shape, bf16),
        ),
        in_specs=[smem, smem, vmem, vmem, vmem, vmem, vmem, hbm, hbm],
        out_specs=(vmem, vmem),
        scratch_shapes=[
            pltpu.VMEM((16, 128, 256), bf16),
            pltpu.VMEM((8, 256, HD), bf16),
        ]
        + [pltpu.VMEM((16, HALF, 256), bf16)] * 7
        + [
            pltpu.VMEM((NZ, 4, 2 * HALF, 256), bf16),
            pltpu.VMEM((NZ, 4, 2 * HALF, 256), bf16),
            pltpu.VMEM((4, 8, 128), jnp.int32),
            pltpu.SMEM((4, 8, 128), jnp.int32),
            pltpu.VMEM((8, 256, HD), f32),
            pltpu.VMEM((8, 256, HD), f32),
            pltpu.VMEM((8, 256, HD), f32),
            pltpu.VMEM((4, 256, HD), bf16),
            pltpu.VMEM((4, 256, HD), bf16),
            pltpu.VMEM((4, 8, 128), f32),
            pltpu.VMEM((4, 8, 128), f32),
            dma((5,)),
            dma((2, 4, CHUNKS)),
            dma((2, 4, CHUNKS)),
            dma((NZ, 4)),
            dma((NZ, 4)),
            dma((4,)),
            dma((4,)),
            dma((4,)),
            dma((4,)),
            dma((4,)),
            dma((4,)),
            dma((4,)),
            dma((4,)),
            dma((4,)),
        ],
        compiler_params=pltpu.CompilerParams(
            collective_id=0, has_side_effects=True, vmem_limit_bytes=56 * 1024 * 1024
        ),
        cost_estimate=pl.CostEstimate(
            flops=5 * 10**9, bytes_accessed=3 * 2**20, transcendentals=10**7
        ),
        name="spanned_attention",
    )(
        hit_owner.reshape(-1),
        hit_slot,
        decode_table.T,
        decode_length,
        decode_query,
        decode_kv,
        span_kv,
        span_query,
        kv_pool,
    )


def solution(mesh):
    placed = (
        P("replica", "tensor"),
        P("replica", "tensor"),
        P("replica", None, "tensor"),
        P("replica", None),
        P("replica"),
        P("replica", "tensor"),
        P("replica", "tensor"),
        P("replica", None),
        P("replica", None),
    )
    return jax.shard_map(
        local,
        mesh=mesh,
        in_specs=placed,
        out_specs=(P("replica", "tensor"), P("replica", "tensor")),
        check_vma=False,
    )
```

```python
import functools
import math

import jax
import jax.numpy as jnp
from jax import lax
from jax.experimental import pallas as pl
from jax.experimental.pallas import tpu as pltpu
from jax.sharding import PartitionSpec as P

MESH = pl.DeviceIdType.MESH
HD = 128
NZ = 8
HALF = 64
CHUNKS = 2
PIECE = HALF // CHUNKS
TILE = 512
SCALE = HD ** (-0.5) * math.log2(math.e)
LOW = -1e30


def nt_dot(a, b):
    return lax.dot_general(a, b, (((1,), (1,)), ((), ())), preferred_element_type=jnp.float32)


def column(row):
    n = row.shape[1]
    eye = lax.broadcasted_iota(jnp.int32, (n, n), 0) == lax.broadcasted_iota(jnp.int32, (n, n), 1)
    return jnp.sum(jnp.where(eye, jnp.broadcast_to(row, (n, n)), 0.0), axis=1, keepdims=True)


def as_row(replicated):
    eye = lax.broadcasted_iota(jnp.int32, (128, 128), 0) == lax.broadcasted_iota(
        jnp.int32, (128, 128), 1
    )
    return jnp.sum(jnp.where(eye, replicated, 0.0), axis=0, keepdims=True)


def kernel(
    owner_s,
    slot_s,
    table_ref,
    length_ref,
    dq_ref,
    dkv_ref,
    skv_ref,
    q_hbm,
    pool_hbm,
    span_out,
    decode_out,
    pool_v,
    qall,
    hop_bufs,
    stage,
    near_stage,
    far_stage,
    far_in,
    inbox,
    tabs,
    tabs_s,
    bundle,
    near,
    near_s,
    keys,
    values,
    scored,
    acc,
    top,
    part_out,
    part_in,
    stat_out,
    stat_in,
    load_sem,
    zsend,
    zrecv,
    psend,
    precv,
    nsend,
    nrecv,
    fsend,
    frecv,
    gsend,
    grecv,
    tsend,
    trecv,
    bsend,
    brecv,
    smem_sem,
    qsend,
    qrecv,
    osend,
    orecv,
    ssend,
    srecv,
):
    r = lax.axis_index("replica")
    t = lax.axis_index("tensor")
    yl, z, c = r // 16, (r // 2) % NZ, r % 2
    xh = t % 2
    tx = t + 1 - 2 * xh

    def plane(step):
        return (z + step + NZ) % NZ

    def peer(e):
        return (yl if e < 2 else 1 - yl), (c if e % 2 == 0 else 1 - c)

    def device(e, step):
        py, pc = peer(e)
        return (py * 16 + plane(step) * 2 + pc, t)

    xid = (r, tx)
    up_down = (1, -1)
    partners = [device(e, 0) for e in range(1, 4)] + [xid]
    partners += [device(e, step) for e in range(4) for step in (1, -1)]
    partners += [device(0, 2), device(0, -2)]

    barrier = pltpu.get_barrier_semaphore()
    for other in partners:
        pl.semaphore_signal(barrier, inc=1, device_id=other, device_id_type=MESH)

    loads = [pltpu.make_async_copy(pool_hbm, pool_v, load_sem.at[0])]
    for h in range(4):
        loads.append(
            pltpu.make_async_copy(
                q_hbm.at[:, pl.ds(h * HD, HD)], qall.at[pl.ds(h * 256, 256)], load_sem.at[1 + h]
            )
        )
    for copy in loads:
        copy.start()

    def remote(src, dst, send, recv, where):
        return pltpu.make_async_remote_copy(
            src_ref=src,
            dst_ref=dst,
            send_sem=send,
            recv_sem=recv,
            device_id=where,
            device_id_type=MESH,
        )

    def ring(d, k, ch):
        if k == 1:
            first = pl.multiple_of(xh * HALF + ch * PIECE, PIECE)
            src = pool_hbm.at[:, pl.ds(first, PIECE), :]
        else:
            src = hop_bufs[d][0][ch]
        return remote(
            src,
            hop_bufs[d][k - 1][ch],
            zsend.at[d, k - 1, ch],
            zrecv.at[d, k - 1, ch],
            device(0, up_down[d]),
        )

    both = [(d, ch) for ch in range(CHUNKS) for d in range(2)]

    pl.semaphore_wait(barrier, len(partners))
    for d, ch in both:
        ring(d, 1, ch).start()

    def query_copy(h):
        return remote(
            q_hbm.at[:, pl.ds(h * HD, HD)],
            qall.at[pl.ds((4 + h) * 256, 256)],
            qsend.at[h],
            qrecv.at[h],
            xid,
        )

    lane = lax.broadcasted_iota(jnp.int32, (8, 128), 1)
    lane_owner, lane_rank = lane // 2, lane % 2

    def note_hit(i, carried):
        table, seen = carried
        match = lane_owner == owner_s[i]
        table = jnp.where(match & (seen == lane_rank), slot_s[i], table)
        return table, seen + match.astype(jnp.int32)

    table, _ = lax.fori_loop(
        0,
        32,
        note_hit,
        (jnp.full((8, 128), -1, jnp.int32), jnp.zeros((8, 128), jnp.int32)),
    )
    tabs[0] = table

    def table_copy(e):
        return remote(tabs.at[0], tabs.at[e], tsend.at[e], trecv.at[e], device(e, 0))

    for e in range(1, 4):
        table_copy(e).start()
    for h in range(4):
        query_copy(h).start()

    steps = (1, 2, -1, -2)

    def bundle_copy(i):
        back = steps.index(-steps[i])
        return remote(bundle, near.at[back], bsend.at[back], brecv.at[back], device(0, steps[i]))

    def bundle_wait(i):
        return remote(bundle, near.at[i], bsend.at[i], brecv.at[i], device(0, steps[i]))

    bundle[...] = jnp.full((8, 128), -1, jnp.int32)
    for e in range(4):
        if e:
            table_copy(e).wait_recv()
        bundle[e : e + 1, :] = tabs[e, 0:1, :]
    for i in range(4):
        bundle_copy(i).start()
    moved = pltpu.make_async_copy(bundle, tabs_s, smem_sem.at[0])
    moved.start()
    loads[0].wait()
    moved.wait()

    def plane_of(p):
        return plane(-p if p < 5 else p - 4)

    def hand_copy(p, ch, e):
        return remote(
            stage.at[p if p < 3 else p - 2, ch, e],
            inbox.at[p, ch, e],
            psend.at[p, ch, e],
            precv.at[p, ch, e],
            device(e, 0),
        )

    def asked(rows_s, e, owner, rank):
        return jnp.clip(rows_s[e, owner * 2 + rank], 0, 15)

    def hand_out(p, ch):
        owner = yl * 16 + plane_of(p) * 2 + c
        for e in (3, 2, 1, 0):
            for rank in range(2):
                slot = asked(tabs_s, e, owner, rank)
                if p == 0:
                    first = pl.multiple_of(xh * HALF + ch * PIECE, PIECE)
                    rows = pool_v[slot, pl.ds(first, PIECE), :]
                else:
                    d, k = (0, p) if p < 5 else (1, p - 4)
                    rows = hop_bufs[d][k - 1][ch][slot]
                place = pl.ds(rank * PIECE, PIECE)
                if e == 0:
                    inbox[p, ch, 0, place, :] = rows
                else:
                    stage[p if p < 3 else p - 2, ch, e, place, :] = rows
            if e:
                hand_copy(p, ch, e).start()

    for ch in range(CHUNKS):
        hand_out(0, ch)

    count = 32
    dq = jnp.concatenate([dq_ref[:, pl.ds(g * HD, HD)] for g in range(4)], axis=0)
    lengths = column(length_ref[...].astype(jnp.float32))
    names = [column(table_ref[b : b + 1, :].astype(jnp.float32)) for b in range(4)]
    spot = lax.broadcasted_iota(jnp.int32, (count, HD), 1).astype(jnp.float32)

    def times(block):
        seen = jnp.zeros((count, HD), jnp.float32)
        for b in range(4):
            limit = jnp.where(names[b] == block, lengths - 128.0 * b, 0.0)
            seen = seen + jnp.where(spot < limit, 1.0, 0.0)
        return jnp.concatenate([seen] * 4, axis=0)

    own_key = jnp.concatenate([dkv_ref[:, :HD].astype(jnp.float32)] * 4, axis=0)
    own_value = jnp.concatenate([dkv_ref[:, HD:].astype(jnp.float32)] * 4, axis=0)
    own_score = jnp.sum(dq.astype(jnp.float32) * own_key, axis=1, keepdims=True)

    def decode_step(it, carried):
        highest, weight_sum, mixture = carried
        rows = pool_v[pl.ds(it * 4, 4)].reshape(4 * HD, 2 * HD)
        scores = nt_dot(dq, rows[:, :HD])
        seen = jnp.concatenate([times((it * 4 + i).astype(jnp.float32)) for i in range(4)], axis=1)
        masked = jnp.where(seen > 0.0, scores, LOW)
        raised = jnp.maximum(highest, jnp.max(masked, axis=1, keepdims=True))
        weights = jnp.exp2((masked - raised) * SCALE)
        shrink = jnp.exp2((highest - raised) * SCALE)
        weight_sum = weight_sum * shrink + jnp.sum(weights * seen, axis=1, keepdims=True)
        spread = (weights.astype(jnp.bfloat16).astype(jnp.float32) * seen).astype(jnp.bfloat16)
        mixture = mixture * shrink + jnp.dot(
            spread, rows[:, HD:], preferred_element_type=jnp.float32
        )
        return raised, weight_sum, mixture

    _, weight_sum, mixture = lax.fori_loop(
        0, 4, decode_step, (own_score, jnp.ones((128, 1), jnp.float32), own_value)
    )
    mixed = (mixture / weight_sum).astype(jnp.bfloat16)
    for g in range(4):
        decode_out[:, pl.ds(g * HD, HD)] = mixed[g * count : (g + 1) * count]

    def forward(ch):
        for d in range(2):
            ring(d, 1, ch).wait_recv()
            ring(d, 2, ch).start()

    forward(0)

    for copy in loads[1:]:
        copy.wait()
    fresh_keys = skv_ref[:, :HD]
    fresh_values = jnp.concatenate([skv_ref[:, HD:], jnp.ones((256, HD), jnp.bfloat16)], axis=1)
    causal = lax.broadcasted_iota(jnp.int32, (256, 256), 0) >= lax.broadcasted_iota(
        jnp.int32, (256, 256), 1
    )

    def fresh_step(h, carried):
        for i in range(2):
            rows = pl.ds(pl.multiple_of((2 * h + i) * 256, 256), 256)
            masked = jnp.where(causal, nt_dot(qall[rows, :], fresh_keys), LOW)
            highest = jnp.broadcast_to(jnp.max(masked, axis=1, keepdims=True), (256, HD))
            weights = jnp.concatenate(
                [
                    jnp.exp2((masked[:, j * HD : (j + 1) * HD] - highest) * SCALE)
                    for j in range(2)
                ],
                axis=1,
            )
            top[rows, :] = highest
            acc[rows, :] = jnp.dot(
                weights.astype(jnp.bfloat16), fresh_values, preferred_element_type=jnp.float32
            )
            rows = pl.ds(pl.multiple_of((4 + 2 * h + i) * 256, 256), 256)
            top[rows, :] = jnp.full((256, HD), LOW, jnp.float32)
            acc[rows, :] = jnp.zeros((256, 2 * HD), jnp.float32)
        return carried

    lax.fori_loop(0, 2, fresh_step, 0)
    forward(1)

    seen_key = jnp.broadcast_to(skv_ref[0:1, :HD].astype(jnp.float32), (PIECE, HD)).astype(
        jnp.bfloat16
    )

    def prepare(p, place):
        for ch in range(CHUNKS):
            for e in range(4):
                py, pc = peer(e)
                owner = py * 16 + plane_of(p) * 2 + pc
                for rank in range(2):
                    used = tabs_s[0, owner * 2 + rank] >= 0
                    cell = inbox[p, ch, e, pl.ds(rank * PIECE, PIECE), :]
                    rows = pl.ds(((ch * 4 + e) * 2 + rank) * PIECE, PIECE)
                    keys[place, rows, :] = jnp.where(used, cell[:, :HD], seen_key)
                    values[place, rows, :HD] = jnp.where(
                        used, cell[:, HD:], jnp.zeros((PIECE, HD), jnp.bfloat16)
                    )
                    values[place, rows, HD:] = jnp.where(
                        used,
                        jnp.ones((PIECE, HD), jnp.bfloat16),
                        jnp.zeros((PIECE, HD), jnp.bfloat16),
                    )

    def tile_rows(tile):
        if isinstance(tile, int):
            return pl.ds(tile * TILE, TILE)
        return pl.ds(pl.multiple_of(tile * TILE, TILE), TILE)

    def score(place, tile, slot):
        scored[slot] = nt_dot(qall[tile_rows(tile), :], keys[place])

    def fold(place, tile, slot):
        rows = tile_rows(tile)
        parts = [scored[slot, :, j * HD : (j + 1) * HD] for j in range(4)]
        highest = top[rows, :]
        most = jnp.maximum(jnp.maximum(parts[0], parts[1]), jnp.maximum(parts[2], parts[3]))
        raised = jnp.maximum(
            highest, jnp.broadcast_to(jnp.max(most, axis=1, keepdims=True), (TILE, HD))
        )
        weights = jnp.concatenate(
            [jnp.exp2((part - raised) * SCALE).astype(jnp.bfloat16) for part in parts], axis=1
        )
        shrink = jnp.exp2((highest - raised) * SCALE)
        top[rows, :] = raised
        gained = jnp.dot(weights, values[place], preferred_element_type=jnp.float32)
        acc[rows, :HD] = acc[rows, :HD] * shrink + gained[:, :HD]
        acc[rows, HD:] = acc[rows, HD:] * shrink + gained[:, HD:]

    def attend(places):
        last = 4 * places - 1
        score(0, 0, 0)

        def two(j, carried):
            i = 2 * j
            score((i + 1) // 4, (i + 1) % 4, 1)
            fold(i // 4, i % 4, 0)
            after = jnp.minimum(i + 2, last)
            score(after // 4, after % 4, 0)
            fold((i + 1) // 4, (i + 1) % 4, 1)
            return carried

        lax.fori_loop(0, 2 * places, two, 0)

    def collect(p):
        for ch in range(CHUNKS):
            for e in range(1, 4):
                hand_copy(p, ch, e).wait_recv()

    for h in range(4):
        query_copy(h).wait_recv()
    for ch in range(CHUNKS):
        hand_out(1, ch)
        hand_out(5, ch)
    collect(0)
    prepare(0, 0)
    attend(1)

    for i in range(4):
        bundle_wait(i).wait_recv()
        moved = pltpu.make_async_copy(near.at[i], near_s.at[i], smem_sem.at[1 + i])
        moved.start()
        moved.wait()

    def near_copy(d, ch, e):
        return remote(
            near_stage.at[d, ch, e],
            inbox.at[(3, 7)[d], ch, e],
            nsend.at[d, ch, e],
            nrecv.at[d, ch, e],
            device(e, up_down[d]),
        )

    def far_copy(d, ch):
        return remote(
            far_stage.at[d, ch],
            far_in.at[d, ch],
            fsend.at[d, ch],
            frecv.at[d, ch],
            device(0, up_down[d]),
        )

    def last_copy(d, ch, e):
        return remote(
            far_in.at[d, ch, e],
            inbox.at[4, ch, e, pl.ds(d * PIECE, PIECE)],
            gsend.at[d, ch, e],
            grecv.at[d, ch, e],
            device(e, up_down[d]),
        )

    for ch in range(CHUNKS):
        for d in range(2):
            ring(d, 2, ch).wait_recv()
            block = hop_bufs[d][1][ch]
            owner = yl * 16 + plane(-2 * up_down[d]) * 2 + c
            for e in range(4):
                far_stage[d, ch, e] = block[asked(near_s.at[2 * d + 1], e, owner, d)]
            far_copy(d, ch).start()
            for e in (3, 2, 1, 0):
                for rank in range(2):
                    slot = asked(near_s.at[2 * d], e, owner, rank)
                    near_stage[d, ch, e, pl.ds(rank * PIECE, PIECE), :] = block[slot]
                near_copy(d, ch, e).start()
        hand_out(2, ch)
        hand_out(6, ch)

    for place, p in enumerate((1, 5)):
        collect(p)
        prepare(p, place)
    attend(2)
    for d, ch in both:
        far_copy(d, ch).wait_recv()
        for e in (3, 2, 1, 0):
            last_copy(d, ch, e).start()
    for place, p in enumerate((2, 6)):
        collect(p)
        prepare(p, place)
    attend(2)
    for d, ch in both:
        for e in range(4):
            near_copy(d, ch, e).wait_recv()
    for place, p in enumerate((3, 7)):
        prepare(p, place)
    attend(2)
    for d, ch in both:
        for e in range(4):
            last_copy(d, ch, e).wait_recv()
    prepare(4, 0)

    def part_copy(i):
        return remote(part_out.at[i], part_in.at[i], osend.at[i], orecv.at[i], xid)

    def stat_copy(i):
        return remote(stat_out.at[i], stat_in.at[i], ssend.at[i], srecv.at[i], xid)

    def hand_back(i):
        base = (2 + i) * TILE
        part_out[i] = acc[pl.ds(base, TILE), :HD].astype(jnp.bfloat16)
        part_copy(i).start()
        for j in range(4):
            rows = pl.ds(base + j * HD, HD)
            stat_out[i, j : j + 1, :] = as_row(top[rows, :])
            stat_out[i, 4 + j : 5 + j, :] = as_row(acc[rows, HD:])
        stat_copy(i).start()

    score(0, 2, 0)
    score(0, 3, 1)
    fold(0, 2, 0)
    hand_back(0)
    score(0, 0, 0)
    fold(0, 3, 1)
    hand_back(1)
    score(0, 1, 1)
    fold(0, 0, 0)
    fold(0, 1, 1)

    for i in range(2):
        part_copy(i).wait_recv()
        stat_copy(i).wait_recv()
        for j in range(4):
            base = i * TILE + j * HD
            rows = pl.ds(base, HD)
            here = top[rows, :]
            there = jnp.broadcast_to(column(stat_in[i, j : j + 1, :]), (HD, HD))
            extra = jnp.broadcast_to(column(stat_in[i, 4 + j : 5 + j, :]), (HD, HD))
            peak = jnp.maximum(here, there)
            keep, take = jnp.exp2((here - peak) * SCALE), jnp.exp2((there - peak) * SCALE)
            sums = acc[rows, HD:] * keep + extra * take
            mixed = acc[rows, :HD] * keep + part_in[i, pl.ds(j * HD, HD), :].astype(
                jnp.float32
            ) * take
            span_out[pl.ds(base % 256, HD), pl.ds(base // 256 * HD, HD)] = (mixed / sums).astype(
                jnp.bfloat16
            )

    for d, ch in both:
        ring(d, 1, ch).wait_send()
        ring(d, 2, ch).wait_send()
        far_copy(d, ch).wait_send()
        for e in range(4):
            near_copy(d, ch, e).wait_send()
            last_copy(d, ch, e).wait_send()
    for i in range(4):
        bundle_copy(i).wait_send()
        query_copy(i).wait_send()
    for i in range(2):
        part_copy(i).wait_send()
        stat_copy(i).wait_send()
    for e in range(1, 4):
        table_copy(e).wait_send()
        for p in (0, 1, 2, 5, 6):
            for ch in range(CHUNKS):
                hand_copy(p, ch, e).wait_send()


def staged(*refs):
    first = 9 + 2 + 2
    flat = refs[first : first + 8]
    bufs = tuple(tuple(tuple(flat[(d * 2 + k) * 2 + ch] for ch in range(2)) for k in range(2)) for d in range(2))
    kernel(*refs[:first], bufs, *refs[first + 8 :])


def local(
    span_query,
    span_kv,
    kv_pool,
    hit_owner,
    hit_slot,
    decode_query,
    decode_kv,
    decode_table,
    decode_length,
):
    vmem = pl.BlockSpec(memory_space=pltpu.VMEM)
    smem = pl.BlockSpec(memory_space=pltpu.SMEM)
    hbm = pl.BlockSpec(memory_space=pl.ANY)
    dma = pltpu.SemaphoreType.DMA
    bf16, f32 = jnp.bfloat16, jnp.float32
    return pl.pallas_call(
        staged,
        out_shape=(
            jax.ShapeDtypeStruct(span_query.shape, bf16),
            jax.ShapeDtypeStruct(decode_query.shape, bf16),
        ),
        in_specs=[smem, smem, vmem, vmem, vmem, vmem, vmem, hbm, hbm],
        out_specs=(vmem, vmem),
        scratch_shapes=[
            pltpu.VMEM((16, 128, 256), bf16),
            pltpu.VMEM((2048, HD), bf16),
        ]
        + [pltpu.VMEM((16, PIECE, 256), bf16)] * 8
        + [
            pltpu.VMEM((5, CHUNKS, 4, 2 * PIECE, 256), bf16),
            pltpu.VMEM((2, CHUNKS, 4, 2 * PIECE, 256), bf16),
            pltpu.VMEM((2, CHUNKS, 4, PIECE, 256), bf16),
            pltpu.VMEM((2, CHUNKS, 4, PIECE, 256), bf16),
            pltpu.VMEM((NZ, CHUNKS, 4, 2 * PIECE, 256), bf16),
            pltpu.VMEM((4, 8, 128), jnp.int32),
            pltpu.SMEM((8, 128), jnp.int32),
            pltpu.VMEM((8, 128), jnp.int32),
            pltpu.VMEM((4, 8, 128), jnp.int32),
            pltpu.SMEM((4, 8, 128), jnp.int32),
            pltpu.VMEM((2, 512, HD), bf16),
            pltpu.VMEM((2, 512, 2 * HD), bf16),
            pltpu.VMEM((2, TILE, 512), f32),
            pltpu.VMEM((2048, 2 * HD), f32),
            pltpu.VMEM((2048, HD), f32),
            pltpu.VMEM((2, TILE, HD), bf16),
            pltpu.VMEM((2, TILE, HD), bf16),
            pltpu.VMEM((2, 8, 128), f32),
            pltpu.VMEM((2, 8, 128), f32),
            dma((5,)),
            dma((2, 2, CHUNKS)),
            dma((2, 2, CHUNKS)),
            dma((NZ, CHUNKS, 4)),
            dma((NZ, CHUNKS, 4)),
            dma((2, CHUNKS, 4)),
            dma((2, CHUNKS, 4)),
            dma((2, CHUNKS)),
            dma((2, CHUNKS)),
            dma((2, CHUNKS, 4)),
            dma((2, CHUNKS, 4)),
            dma((4,)),
            dma((4,)),
            dma((4,)),
            dma((4,)),
            dma((5,)),
            dma((4,)),
            dma((4,)),
            dma((2,)),
            dma((2,)),
            dma((2,)),
            dma((2,)),
        ],
        compiler_params=pltpu.CompilerParams(
            collective_id=0, has_side_effects=True, vmem_limit_bytes=56 * 1024 * 1024
        ),
        cost_estimate=pl.CostEstimate(
            flops=5 * 10**9, bytes_accessed=3 * 2**20, transcendentals=10**7
        ),
        name="spanned_attention",
    )(
        hit_owner.reshape(-1),
        hit_slot,
        decode_table.T,
        decode_length,
        decode_query,
        decode_kv,
        span_kv,
        span_query,
        kv_pool,
    )


def solution(mesh):
    placed = (
        P("replica", "tensor"),
        P("replica", "tensor"),
        P("replica", None, "tensor"),
        P("replica", None),
        P("replica"),
        P("replica", "tensor"),
        P("replica", "tensor"),
        P("replica", None),
        P("replica", None),
    )
    return jax.shard_map(
        local,
        mesh=mesh,
        in_specs=placed,
        out_specs=(P("replica", "tensor"), P("replica", "tensor")),
        check_vma=False,
    )
```

```python
import functools
import math

import jax
import jax.numpy as jnp
from jax import lax
from jax.experimental import pallas as pl
from jax.experimental.pallas import tpu as pltpu
from jax.sharding import PartitionSpec as P

MESH = pl.DeviceIdType.MESH
HD = 128
NZ = 8
HALF = 64
CHUNKS = 2
PIECE = HALF // CHUNKS
TILE = 512
SCALE = HD ** (-0.5) * math.log2(math.e)
LOW = -1e30


def nt_dot(a, b):
    return lax.dot_general(a, b, (((1,), (1,)), ((), ())), preferred_element_type=jnp.float32)


def column(row):
    n = row.shape[1]
    eye = lax.broadcasted_iota(jnp.int32, (n, n), 0) == lax.broadcasted_iota(jnp.int32, (n, n), 1)
    return jnp.sum(jnp.where(eye, jnp.broadcast_to(row, (n, n)), 0.0), axis=1, keepdims=True)


def as_row(replicated):
    eye = lax.broadcasted_iota(jnp.int32, (128, 128), 0) == lax.broadcasted_iota(
        jnp.int32, (128, 128), 1
    )
    return jnp.sum(jnp.where(eye, replicated, 0.0), axis=0, keepdims=True)


def kernel(
    owner_hbm,
    slot_hbm,
    table_hbm,
    length_hbm,
    dq_hbm,
    dkv_hbm,
    skv_hbm,
    q_hbm,
    pool_hbm,
    span_hbm,
    decode_hbm,
    owner_s,
    slot_s,
    table_ref,
    length_ref,
    dq_ref,
    dkv_ref,
    skv_ref,
    span_out,
    decode_out,
    pool_v,
    qall,
    hop_bufs,
    stage,
    near_stage,
    far_stage,
    far_in,
    inbox,
    tabs,
    tabs_s,
    bundle,
    near,
    near_s,
    keys,
    values,
    scored,
    acc,
    top,
    part_out,
    part_in,
    stat_out,
    stat_in,
    load_sem,
    store_sem,
    zsend,
    zrecv,
    psend,
    precv,
    nsend,
    nrecv,
    fsend,
    frecv,
    gsend,
    grecv,
    tsend,
    trecv,
    bsend,
    brecv,
    smem_sem,
    qsend,
    qrecv,
    osend,
    orecv,
    ssend,
    srecv,
):
    r = lax.axis_index("replica")
    t = lax.axis_index("tensor")
    yl, z, c = r // 16, (r // 2) % NZ, r % 2
    xh = t % 2
    tx = t + 1 - 2 * xh

    def plane(step):
        return (z + step + NZ) % NZ

    def peer(e):
        return (yl if e < 2 else 1 - yl), (c if e % 2 == 0 else 1 - c)

    def device(e, step):
        py, pc = peer(e)
        return (py * 16 + plane(step) * 2 + pc, t)

    xid = (r, tx)
    up_down = (1, -1)
    partners = [device(e, 0) for e in range(1, 4)] + [xid]
    partners += [device(e, step) for e in range(4) for step in (1, -1)]
    partners += [device(0, 2), device(0, -2)]

    barrier = pltpu.get_barrier_semaphore()
    for other in partners:
        pl.semaphore_signal(barrier, inc=1, device_id=other, device_id_type=MESH)

    pairs = [
        (owner_hbm, owner_s),
        (slot_hbm, slot_s),
        (pool_hbm, pool_v),
        (table_hbm, table_ref),
        (length_hbm, length_ref),
        (dq_hbm, dq_ref),
        (dkv_hbm, dkv_ref),
        (skv_hbm, skv_ref),
    ]
    for h in range(4):
        pairs.append((q_hbm.at[:, pl.ds(h * HD, HD)], qall.at[pl.ds(h * 256, 256)]))
    loads = [pltpu.make_async_copy(src, dst, load_sem.at[i]) for i, (src, dst) in enumerate(pairs)]

    def remote(src, dst, send, recv, where):
        return pltpu.make_async_remote_copy(
            src_ref=src,
            dst_ref=dst,
            send_sem=send,
            recv_sem=recv,
            device_id=where,
            device_id_type=MESH,
        )

    def ring(d, k, ch):
        if k == 1:
            first = pl.multiple_of(xh * HALF + ch * PIECE, PIECE)
            src = pool_hbm.at[:, pl.ds(first, PIECE), :]
        else:
            src = hop_bufs[d][0][ch]
        return remote(
            src,
            hop_bufs[d][k - 1][ch],
            zsend.at[d, k - 1, ch],
            zrecv.at[d, k - 1, ch],
            device(0, up_down[d]),
        )

    both = [(d, ch) for ch in range(CHUNKS) for d in range(2)]

    pl.semaphore_wait(barrier, len(partners))
    for d, ch in both:
        ring(d, 1, ch).start()
    for copy in loads:
        copy.start()

    def query_copy(h):
        return remote(
            q_hbm.at[:, pl.ds(h * HD, HD)],
            qall.at[pl.ds((4 + h) * 256, 256)],
            qsend.at[h],
            qrecv.at[h],
            xid,
        )

    for copy in loads[:2]:
        copy.wait()

    lane = lax.broadcasted_iota(jnp.int32, (8, 128), 1)
    lane_owner, lane_rank = lane // 2, lane % 2

    def note_hit(i, carried):
        table, seen = carried
        match = lane_owner == owner_s[i]
        table = jnp.where(match & (seen == lane_rank), slot_s[i], table)
        return table, seen + match.astype(jnp.int32)

    table, _ = lax.fori_loop(
        0,
        32,
        note_hit,
        (jnp.full((8, 128), -1, jnp.int32), jnp.zeros((8, 128), jnp.int32)),
    )
    tabs[0] = table

    def table_copy(e):
        return remote(tabs.at[0], tabs.at[e], tsend.at[e], trecv.at[e], device(e, 0))

    for e in range(1, 4):
        table_copy(e).start()
    for h in range(4):
        query_copy(h).start()

    for copy in loads[2:7]:
        copy.wait()
    count = 32
    dq = jnp.concatenate([dq_ref[:, pl.ds(g * HD, HD)] for g in range(4)], axis=0)
    lengths = column(length_ref[...].astype(jnp.float32))
    names = [column(table_ref[b : b + 1, :].astype(jnp.float32)) for b in range(4)]
    spot = lax.broadcasted_iota(jnp.int32, (count, HD), 1).astype(jnp.float32)

    def times(block):
        seen = jnp.zeros((count, HD), jnp.float32)
        for b in range(4):
            limit = jnp.where(names[b] == block, lengths - 128.0 * b, 0.0)
            seen = seen + jnp.where(spot < limit, 1.0, 0.0)
        return jnp.concatenate([seen] * 4, axis=0)

    own_key = jnp.concatenate([dkv_ref[:, :HD].astype(jnp.float32)] * 4, axis=0)
    own_value = jnp.concatenate([dkv_ref[:, HD:].astype(jnp.float32)] * 4, axis=0)
    own_score = jnp.sum(dq.astype(jnp.float32) * own_key, axis=1, keepdims=True)

    def decode_step(it, carried):
        highest, weight_sum, mixture = carried
        rows = pool_v[pl.ds(it * 4, 4)].reshape(4 * HD, 2 * HD)
        scores = nt_dot(dq, rows[:, :HD])
        seen = jnp.concatenate([times((it * 4 + i).astype(jnp.float32)) for i in range(4)], axis=1)
        masked = jnp.where(seen > 0.0, scores, LOW)
        raised = jnp.maximum(highest, jnp.max(masked, axis=1, keepdims=True))
        weights = jnp.exp2((masked - raised) * SCALE)
        shrink = jnp.exp2((highest - raised) * SCALE)
        weight_sum = weight_sum * shrink + jnp.sum(weights * seen, axis=1, keepdims=True)
        spread = (weights.astype(jnp.bfloat16).astype(jnp.float32) * seen).astype(jnp.bfloat16)
        mixture = mixture * shrink + jnp.dot(
            spread, rows[:, HD:], preferred_element_type=jnp.float32
        )
        return raised, weight_sum, mixture

    _, weight_sum, mixture = lax.fori_loop(
        0, 4, decode_step, (own_score, jnp.ones((128, 1), jnp.float32), own_value)
    )
    mixed = (mixture / weight_sum).astype(jnp.bfloat16)
    for g in range(4):
        decode_out[:, pl.ds(g * HD, HD)] = mixed[g * count : (g + 1) * count]
    decoded = pltpu.make_async_copy(decode_out, decode_hbm, store_sem.at[0])
    decoded.start()

    steps = (1, 2, -1, -2)

    def bundle_copy(i):
        back = steps.index(-steps[i])
        return remote(bundle, near.at[back], bsend.at[back], brecv.at[back], device(0, steps[i]))

    def bundle_wait(i):
        return remote(bundle, near.at[i], bsend.at[i], brecv.at[i], device(0, steps[i]))

    bundle[...] = jnp.full((8, 128), -1, jnp.int32)
    for e in range(4):
        if e:
            table_copy(e).wait_recv()
        bundle[e : e + 1, :] = tabs[e, 0:1, :]
    for i in range(4):
        bundle_copy(i).start()
    moved = pltpu.make_async_copy(bundle, tabs_s, smem_sem.at[0])
    moved.start()
    moved.wait()

    def plane_of(p):
        return plane(-p if p < 5 else p - 4)

    def hand_copy(p, ch, e):
        return remote(
            stage.at[p if p < 3 else p - 2, ch, e],
            inbox.at[p, ch, e],
            psend.at[p, ch, e],
            precv.at[p, ch, e],
            device(e, 0),
        )

    def asked(rows_s, e, owner, rank):
        return jnp.clip(rows_s[e, owner * 2 + rank], 0, 15)

    def hand_out(p, ch):
        owner = yl * 16 + plane_of(p) * 2 + c
        for e in (3, 2, 1, 0):
            for rank in range(2):
                slot = asked(tabs_s, e, owner, rank)
                if p == 0:
                    first = pl.multiple_of(xh * HALF + ch * PIECE, PIECE)
                    rows = pool_v[slot, pl.ds(first, PIECE), :]
                else:
                    d, k = (0, p) if p < 5 else (1, p - 4)
                    rows = hop_bufs[d][k - 1][ch][slot]
                place = pl.ds(rank * PIECE, PIECE)
                if e == 0:
                    inbox[p, ch, 0, place, :] = rows
                else:
                    stage[p if p < 3 else p - 2, ch, e, place, :] = rows
            if e:
                hand_copy(p, ch, e).start()

    for ch in range(CHUNKS):
        hand_out(0, ch)

    def forward(ch):
        for d in range(2):
            ring(d, 1, ch).wait_recv()
            ring(d, 2, ch).start()

    forward(0)
    hand_out(1, 0)
    hand_out(5, 0)

    for copy in loads[7:]:
        copy.wait()
    fresh_keys = skv_ref[:, :HD]
    fresh_values = jnp.concatenate([skv_ref[:, HD:], jnp.ones((256, HD), jnp.bfloat16)], axis=1)
    causal = lax.broadcasted_iota(jnp.int32, (256, 256), 0) >= lax.broadcasted_iota(
        jnp.int32, (256, 256), 1
    )

    def fresh_step(h, carried):
        for i in range(2):
            rows = pl.ds(pl.multiple_of((2 * h + i) * 256, 256), 256)
            masked = jnp.where(causal, nt_dot(qall[rows, :], fresh_keys), LOW)
            highest = jnp.broadcast_to(jnp.max(masked, axis=1, keepdims=True), (256, HD))
            weights = jnp.concatenate(
                [
                    jnp.exp2((masked[:, j * HD : (j + 1) * HD] - highest) * SCALE)
                    for j in range(2)
                ],
                axis=1,
            )
            top[rows, :] = highest
            acc[rows, :] = jnp.dot(
                weights.astype(jnp.bfloat16), fresh_values, preferred_element_type=jnp.float32
            )
            rows = pl.ds(pl.multiple_of((4 + 2 * h + i) * 256, 256), 256)
            top[rows, :] = jnp.full((256, HD), LOW, jnp.float32)
            acc[rows, :] = jnp.zeros((256, 2 * HD), jnp.float32)
        return carried

    lax.fori_loop(0, 2, fresh_step, 0)
    forward(1)
    hand_out(1, 1)
    hand_out(5, 1)

    seen_key = jnp.broadcast_to(skv_ref[0:1, :HD].astype(jnp.float32), (PIECE, HD)).astype(
        jnp.bfloat16
    )

    def prepare(unit, place):
        for i, (p, ch) in enumerate(unit):
            for e in range(4):
                py, pc = peer(e)
                owner = py * 16 + plane_of(p) * 2 + pc
                for rank in range(2):
                    used = tabs_s[0, owner * 2 + rank] >= 0
                    cell = inbox[p, ch, e, pl.ds(rank * PIECE, PIECE), :]
                    rows = pl.ds(((i * 4 + e) * 2 + rank) * PIECE, PIECE)
                    keys[place, rows, :] = jnp.where(used, cell[:, :HD], seen_key)
                    values[place, rows, :HD] = jnp.where(
                        used, cell[:, HD:], jnp.zeros((PIECE, HD), jnp.bfloat16)
                    )
                    values[place, rows, HD:] = jnp.where(
                        used,
                        jnp.ones((PIECE, HD), jnp.bfloat16),
                        jnp.zeros((PIECE, HD), jnp.bfloat16),
                    )

    def whole(p):
        return [(p, ch) for ch in range(CHUNKS)]

    def tile_rows(tile):
        if isinstance(tile, int):
            return pl.ds(tile * TILE, TILE)
        return pl.ds(pl.multiple_of(tile * TILE, TILE), TILE)

    def score(place, tile, slot):
        scored[slot] = nt_dot(qall[tile_rows(tile), :], keys[place])

    def fold(place, tile, slot):
        rows = tile_rows(tile)
        parts = [scored[slot, :, j * HD : (j + 1) * HD] for j in range(4)]
        highest = top[rows, :]
        most = jnp.maximum(jnp.maximum(parts[0], parts[1]), jnp.maximum(parts[2], parts[3]))
        raised = jnp.maximum(
            highest, jnp.broadcast_to(jnp.max(most, axis=1, keepdims=True), (TILE, HD))
        )
        weights = jnp.concatenate(
            [jnp.exp2((part - raised) * SCALE).astype(jnp.bfloat16) for part in parts], axis=1
        )
        shrink = jnp.exp2((highest - raised) * SCALE)
        top[rows, :] = raised
        gained = jnp.dot(weights, values[place], preferred_element_type=jnp.float32)
        acc[rows, :HD] = acc[rows, :HD] * shrink + gained[:, :HD]
        acc[rows, HD:] = acc[rows, HD:] * shrink + gained[:, HD:]

    def attend(places):
        last = 4 * places - 1
        score(0, 0, 0)

        def two(j, carried):
            i = 2 * j
            score((i + 1) // 4, (i + 1) % 4, 1)
            fold(i // 4, i % 4, 0)
            after = jnp.minimum(i + 2, last)
            score(after // 4, after % 4, 0)
            fold((i + 1) // 4, (i + 1) % 4, 1)
            return carried

        lax.fori_loop(0, 2 * places, two, 0)

    both_chunks = tuple(range(CHUNKS))

    def collect(p, chunks):
        for ch in chunks:
            for e in range(1, 4):
                hand_copy(p, ch, e).wait_recv()

    for h in range(4):
        query_copy(h).wait_recv()
    collect(0, both_chunks)
    prepare(whole(0), 0)
    attend(1)

    for i in range(4):
        bundle_wait(i).wait_recv()
        moved = pltpu.make_async_copy(near.at[i], near_s.at[i], smem_sem.at[1 + i])
        moved.start()
        moved.wait()

    def near_copy(d, ch, e):
        return remote(
            near_stage.at[d, ch, e],
            inbox.at[(3, 7)[d], ch, e],
            nsend.at[d, ch, e],
            nrecv.at[d, ch, e],
            device(e, up_down[d]),
        )

    def far_copy(d, ch):
        return remote(
            far_stage.at[d, ch],
            far_in.at[d, ch],
            fsend.at[d, ch],
            frecv.at[d, ch],
            device(0, up_down[d]),
        )

    def last_copy(d, ch, e):
        return remote(
            far_in.at[d, ch, e],
            inbox.at[4, ch, e, pl.ds(d * PIECE, PIECE)],
            gsend.at[d, ch, e],
            grecv.at[d, ch, e],
            device(e, up_down[d]),
        )

    def send_far(ch):
        for d in range(2):
            ring(d, 2, ch).wait_recv()
            block = hop_bufs[d][1][ch]
            owner = yl * 16 + plane(-2 * up_down[d]) * 2 + c
            for e in range(4):
                far_stage[d, ch, e] = block[asked(near_s.at[2 * d + 1], e, owner, d)]
            far_copy(d, ch).start()

    def send_near(ch):
        for d in range(2):
            block = hop_bufs[d][1][ch]
            owner = yl * 16 + plane(-2 * up_down[d]) * 2 + c
            for e in (3, 2, 1, 0):
                for rank in range(2):
                    slot = asked(near_s.at[2 * d], e, owner, rank)
                    near_stage[d, ch, e, pl.ds(rank * PIECE, PIECE), :] = block[slot]
                near_copy(d, ch, e).start()

    send_far(0)
    send_near(0)
    hand_out(2, 0)
    hand_out(6, 0)
    for place, p in enumerate((1, 5)):
        collect(p, both_chunks)
        prepare(whole(p), place)
    attend(2)
    send_far(1)
    send_near(1)
    hand_out(2, 1)
    hand_out(6, 1)

    def forward_far(ch):
        for d in range(2):
            far_copy(d, ch).wait_recv()
            for e in (3, 2, 1, 0):
                last_copy(d, ch, e).start()

    def pair_unit(p, ch):
        unit = [(p, ch), (p + 4, ch)]
        if p < 3:
            for q, _ in unit:
                collect(q, (ch,))
        else:
            for d in range(2):
                for e in range(4):
                    near_copy(d, ch, e).wait_recv()
        prepare(unit, 0)
        attend(1)

    forward_far(0)
    pair_unit(2, 0)
    forward_far(1)
    pair_unit(2, 1)
    pair_unit(3, 0)
    pair_unit(3, 1)
    for d, ch in both:
        for e in range(4):
            last_copy(d, ch, e).wait_recv()
    prepare(whole(4), 0)

    def part_copy(i):
        return remote(part_out.at[i], part_in.at[i], osend.at[i], orecv.at[i], xid)

    def stat_copy(i):
        return remote(stat_out.at[i], stat_in.at[i], ssend.at[i], srecv.at[i], xid)

    def hand_back(i):
        base = (2 + i) * TILE
        part_out[i] = acc[pl.ds(base, TILE), :HD].astype(jnp.bfloat16)
        part_copy(i).start()
        for j in range(4):
            rows = pl.ds(base + j * HD, HD)
            stat_out[i, j : j + 1, :] = as_row(top[rows, :])
            stat_out[i, 4 + j : 5 + j, :] = as_row(acc[rows, HD:])
        stat_copy(i).start()

    score(0, 2, 0)
    score(0, 3, 1)
    fold(0, 2, 0)
    hand_back(0)
    score(0, 0, 0)
    fold(0, 3, 1)
    hand_back(1)
    score(0, 1, 1)
    fold(0, 0, 0)
    fold(0, 1, 1)

    stored = [decoded]
    for i in range(2):
        part_copy(i).wait_recv()
        stat_copy(i).wait_recv()
        for j in range(4):
            base = i * TILE + j * HD
            rows = pl.ds(base, HD)
            here = top[rows, :]
            there = jnp.broadcast_to(column(stat_in[i, j : j + 1, :]), (HD, HD))
            extra = jnp.broadcast_to(column(stat_in[i, 4 + j : 5 + j, :]), (HD, HD))
            peak = jnp.maximum(here, there)
            keep, take = jnp.exp2((here - peak) * SCALE), jnp.exp2((there - peak) * SCALE)
            sums = acc[rows, HD:] * keep + extra * take
            mixed = acc[rows, :HD] * keep + part_in[i, pl.ds(j * HD, HD), :].astype(
                jnp.float32
            ) * take
            span_out[pl.ds(base % 256, HD), pl.ds(base // 256 * HD, HD)] = (mixed / sums).astype(
                jnp.bfloat16
            )
            if j % 2:
                h = 2 * i + j // 2
                stored.append(
                    pltpu.make_async_copy(
                        span_out.at[:, pl.ds(h * HD, HD)],
                        span_hbm.at[:, pl.ds(h * HD, HD)],
                        store_sem.at[1 + h],
                    )
                )
                stored[-1].start()

    for d, ch in both:
        ring(d, 1, ch).wait_send()
        ring(d, 2, ch).wait_send()
        far_copy(d, ch).wait_send()
        for e in range(4):
            near_copy(d, ch, e).wait_send()
            last_copy(d, ch, e).wait_send()
    for i in range(4):
        bundle_copy(i).wait_send()
        query_copy(i).wait_send()
    for i in range(2):
        part_copy(i).wait_send()
        stat_copy(i).wait_send()
    for e in range(1, 4):
        table_copy(e).wait_send()
        for p in (0, 1, 2, 5, 6):
            for ch in range(CHUNKS):
                hand_copy(p, ch, e).wait_send()
    for copy in stored:
        copy.wait()


def staged(*refs):
    first = 9 + 2 + 9 + 2
    flat = refs[first : first + 8]
    bufs = tuple(tuple(tuple(flat[(d * 2 + k) * 2 + ch] for ch in range(2)) for k in range(2)) for d in range(2))
    kernel(*refs[:first], bufs, *refs[first + 8 :])


def place_results(span_ref, decode_ref, span_out, decode_out):
    span_out[...] = span_ref[...]
    decode_out[...] = decode_ref[...]


def local(
    span_query,
    span_kv,
    kv_pool,
    hit_owner,
    hit_slot,
    decode_query,
    decode_kv,
    decode_table,
    decode_length,
):
    hbm = pl.BlockSpec(memory_space=pl.ANY)
    dma = pltpu.SemaphoreType.DMA
    bf16, f32 = jnp.bfloat16, jnp.float32
    results = pl.pallas_call(
        staged,
        out_shape=(
            jax.ShapeDtypeStruct(span_query.shape, bf16),
            jax.ShapeDtypeStruct(decode_query.shape, bf16),
        ),
        in_specs=[hbm] * 9,
        out_specs=(hbm, hbm),
        scratch_shapes=[
            pltpu.SMEM((32,), jnp.int32),
            pltpu.SMEM((32,), jnp.int32),
            pltpu.VMEM((4, 32), jnp.int32),
            pltpu.VMEM((1, 32), jnp.int32),
            pltpu.VMEM(decode_query.shape, bf16),
            pltpu.VMEM(decode_kv.shape, bf16),
            pltpu.VMEM(span_kv.shape, bf16),
            pltpu.VMEM(span_query.shape, bf16),
            pltpu.VMEM(decode_query.shape, bf16),
            pltpu.VMEM((16, 128, 256), bf16),
            pltpu.VMEM((2048, HD), bf16),
        ]
        + [pltpu.VMEM((16, PIECE, 256), bf16)] * 8
        + [
            pltpu.VMEM((5, CHUNKS, 4, 2 * PIECE, 256), bf16),
            pltpu.VMEM((2, CHUNKS, 4, 2 * PIECE, 256), bf16),
            pltpu.VMEM((2, CHUNKS, 4, PIECE, 256), bf16),
            pltpu.VMEM((2, CHUNKS, 4, PIECE, 256), bf16),
            pltpu.VMEM((NZ, CHUNKS, 4, 2 * PIECE, 256), bf16),
            pltpu.VMEM((4, 8, 128), jnp.int32),
            pltpu.SMEM((8, 128), jnp.int32),
            pltpu.VMEM((8, 128), jnp.int32),
            pltpu.VMEM((4, 8, 128), jnp.int32),
            pltpu.SMEM((4, 8, 128), jnp.int32),
            pltpu.VMEM((2, 512, HD), bf16),
            pltpu.VMEM((2, 512, 2 * HD), bf16),
            pltpu.VMEM((2, TILE, 512), f32),
            pltpu.VMEM((2048, 2 * HD), f32),
            pltpu.VMEM((2048, HD), f32),
            pltpu.VMEM((2, TILE, HD), bf16),
            pltpu.VMEM((2, TILE, HD), bf16),
            pltpu.VMEM((2, 8, 128), f32),
            pltpu.VMEM((2, 8, 128), f32),
            dma((12,)),
            dma((5,)),
            dma((2, 2, CHUNKS)),
            dma((2, 2, CHUNKS)),
            dma((NZ, CHUNKS, 4)),
            dma((NZ, CHUNKS, 4)),
            dma((2, CHUNKS, 4)),
            dma((2, CHUNKS, 4)),
            dma((2, CHUNKS)),
            dma((2, CHUNKS)),
            dma((2, CHUNKS, 4)),
            dma((2, CHUNKS, 4)),
            dma((4,)),
            dma((4,)),
            dma((4,)),
            dma((4,)),
            dma((5,)),
            dma((4,)),
            dma((4,)),
            dma((2,)),
            dma((2,)),
            dma((2,)),
            dma((2,)),
        ],
        compiler_params=pltpu.CompilerParams(
            collective_id=0, has_side_effects=True, vmem_limit_bytes=56 * 1024 * 1024
        ),
        cost_estimate=pl.CostEstimate(
            flops=5 * 10**9, bytes_accessed=3 * 2**20, transcendentals=10**7
        ),
        name="spanned_attention",
    )(
        hit_owner.reshape(-1),
        hit_slot,
        decode_table.T,
        decode_length,
        decode_query,
        decode_kv,
        span_kv,
        span_query,
        kv_pool,
    )
    vmem = pl.BlockSpec(memory_space=pltpu.VMEM)
    return pl.pallas_call(
        place_results,
        out_shape=(
            jax.ShapeDtypeStruct(span_query.shape, bf16),
            jax.ShapeDtypeStruct(decode_query.shape, bf16),
        ),
        in_specs=[vmem] * 2,
        out_specs=(vmem,) * 2,
        name="place_results",
    )(*results)


def solution(mesh):
    placed = (
        P("replica", "tensor"),
        P("replica", "tensor"),
        P("replica", None, "tensor"),
        P("replica", None),
        P("replica"),
        P("replica", "tensor"),
        P("replica", "tensor"),
        P("replica", None),
        P("replica", None),
    )
    return jax.shard_map(
        local,
        mesh=mesh,
        in_specs=placed,
        out_specs=(P("replica", "tensor"), P("replica", "tensor")),
        check_vma=False,
    )
```

```python
import functools
import math

import jax
import jax.numpy as jnp
from jax import lax
from jax.experimental import pallas as pl
from jax.experimental.pallas import tpu as pltpu
from jax.sharding import PartitionSpec as P

MESH = pl.DeviceIdType.MESH
HD = 128
NZ = 8
HALF = 64
CHUNKS = 2
PIECE = HALF // CHUNKS
TILE = 512
SCALE = HD ** (-0.5) * math.log2(math.e)
LOW = -1e30


def nt_dot(a, b):
    return lax.dot_general(a, b, (((1,), (1,)), ((), ())), preferred_element_type=jnp.float32)


def column(row):
    n = row.shape[1]
    eye = lax.broadcasted_iota(jnp.int32, (n, n), 0) == lax.broadcasted_iota(jnp.int32, (n, n), 1)
    return jnp.sum(jnp.where(eye, jnp.broadcast_to(row, (n, n)), 0.0), axis=1, keepdims=True)


def as_row(replicated):
    eye = lax.broadcasted_iota(jnp.int32, (128, 128), 0) == lax.broadcasted_iota(
        jnp.int32, (128, 128), 1
    )
    return jnp.sum(jnp.where(eye, replicated, 0.0), axis=0, keepdims=True)


def kernel(
    owner_hbm,
    slot_hbm,
    table_hbm,
    length_hbm,
    dq_hbm,
    dkv_hbm,
    skv_hbm,
    q_hbm,
    pool_hbm,
    span_hbm,
    decode_hbm,
    owner_s,
    slot_s,
    table_ref,
    length_ref,
    dq_ref,
    dkv_ref,
    skv_ref,
    span_out,
    decode_out,
    pool_v,
    qall,
    hop_bufs,
    stage,
    near_stage,
    far_stage,
    far_in,
    inbox,
    tabs,
    tabs_s,
    bundle,
    near,
    near_s,
    keys,
    values,
    scored,
    acc,
    top,
    part_out,
    part_in,
    stat_out,
    stat_in,
    load_sem,
    store_sem,
    zsend,
    zrecv,
    psend,
    precv,
    nsend,
    nrecv,
    fsend,
    frecv,
    gsend,
    grecv,
    tsend,
    trecv,
    bsend,
    brecv,
    smem_sem,
    qsend,
    qrecv,
    osend,
    orecv,
    ssend,
    srecv,
):
    r = lax.axis_index("replica")
    t = lax.axis_index("tensor")
    yl, z, c = r // 16, (r // 2) % NZ, r % 2
    xh = t % 2
    tx = t + 1 - 2 * xh

    def plane(step):
        return (z + step + NZ) % NZ

    def peer(e):
        return (yl if e < 2 else 1 - yl), (c if e % 2 == 0 else 1 - c)

    def device(e, step):
        py, pc = peer(e)
        return (py * 16 + plane(step) * 2 + pc, t)

    xid = (r, tx)
    up_down = (1, -1)
    partners = [device(e, 0) for e in range(1, 4)] + [xid]
    partners += [device(e, step) for e in range(4) for step in (1, -1)]
    partners += [device(0, 2), device(0, -2)]

    barrier = pltpu.get_barrier_semaphore()
    for other in partners:
        pl.semaphore_signal(barrier, inc=1, device_id=other, device_id_type=MESH)

    pairs = [
        (owner_hbm, owner_s),
        (slot_hbm, slot_s),
        (pool_hbm, pool_v),
        (table_hbm, table_ref),
        (length_hbm, length_ref),
        (dq_hbm, dq_ref),
        (dkv_hbm, dkv_ref),
        (skv_hbm, skv_ref),
    ]
    for h in range(4):
        pairs.append((q_hbm.at[:, pl.ds(h * HD, HD)], qall.at[pl.ds(h * 256, 256)]))
    loads = [pltpu.make_async_copy(src, dst, load_sem.at[i]) for i, (src, dst) in enumerate(pairs)]

    def remote(src, dst, send, recv, where):
        return pltpu.make_async_remote_copy(
            src_ref=src,
            dst_ref=dst,
            send_sem=send,
            recv_sem=recv,
            device_id=where,
            device_id_type=MESH,
        )

    def ring(d, k, ch):
        if k == 1:
            first = pl.multiple_of(xh * HALF + ch * PIECE, PIECE)
            src = pool_hbm.at[:, pl.ds(first, PIECE), :]
        else:
            src = hop_bufs[d][0][ch]
        return remote(
            src,
            hop_bufs[d][k - 1][ch],
            zsend.at[d, k - 1, ch],
            zrecv.at[d, k - 1, ch],
            device(0, up_down[d]),
        )

    both = [(d, ch) for ch in range(CHUNKS) for d in range(2)]

    pl.semaphore_wait(barrier, len(partners))
    for d, ch in both:
        ring(d, 1, ch).start()
    for copy in loads:
        copy.start()

    def query_copy(h):
        return remote(
            q_hbm.at[:, pl.ds(h * HD, HD)],
            qall.at[pl.ds((4 + h) * 256, 256)],
            qsend.at[h],
            qrecv.at[h],
            xid,
        )

    for copy in loads[:2]:
        copy.wait()

    lane = lax.broadcasted_iota(jnp.int32, (8, 128), 1)
    lane_owner, lane_rank = lane // 2, lane % 2

    def note_hit(i, carried):
        table, seen = carried
        match = lane_owner == owner_s[i]
        table = jnp.where(match & (seen == lane_rank), slot_s[i], table)
        return table, seen + match.astype(jnp.int32)

    table, _ = lax.fori_loop(
        0,
        32,
        note_hit,
        (jnp.full((8, 128), -1, jnp.int32), jnp.zeros((8, 128), jnp.int32)),
    )
    tabs[0] = table

    def table_copy(e):
        return remote(tabs.at[0], tabs.at[e], tsend.at[e], trecv.at[e], device(e, 0))

    for e in range(1, 4):
        table_copy(e).start()
    for h in range(4):
        query_copy(h).start()

    for copy in loads[2:7]:
        copy.wait()
    count = 32
    dq = jnp.concatenate([dq_ref[:, pl.ds(g * HD, HD)] for g in range(4)], axis=0)
    lengths = column(length_ref[...].astype(jnp.float32))
    names = [column(table_ref[b : b + 1, :].astype(jnp.float32)) for b in range(4)]
    spot = lax.broadcasted_iota(jnp.int32, (count, HD), 1).astype(jnp.float32)

    def times(block):
        seen = jnp.zeros((count, HD), jnp.float32)
        for b in range(4):
            limit = jnp.where(names[b] == block, lengths - 128.0 * b, 0.0)
            seen = seen + jnp.where(spot < limit, 1.0, 0.0)
        return jnp.concatenate([seen] * 4, axis=0)

    own_key = jnp.concatenate([dkv_ref[:, :HD].astype(jnp.float32)] * 4, axis=0)
    own_value = jnp.concatenate([dkv_ref[:, HD:].astype(jnp.float32)] * 4, axis=0)
    own_score = jnp.sum(dq.astype(jnp.float32) * own_key, axis=1, keepdims=True)

    def decode_step(it, carried):
        highest, weight_sum, mixture = carried
        rows = pool_v[pl.ds(it * 4, 4)].reshape(4 * HD, 2 * HD)
        scores = nt_dot(dq, rows[:, :HD])
        seen = jnp.concatenate([times((it * 4 + i).astype(jnp.float32)) for i in range(4)], axis=1)
        masked = jnp.where(seen > 0.0, scores, LOW)
        raised = jnp.maximum(highest, jnp.max(masked, axis=1, keepdims=True))
        weights = jnp.exp2((masked - raised) * SCALE)
        shrink = jnp.exp2((highest - raised) * SCALE)
        weight_sum = weight_sum * shrink + jnp.sum(weights * seen, axis=1, keepdims=True)
        spread = (weights.astype(jnp.bfloat16).astype(jnp.float32) * seen).astype(jnp.bfloat16)
        mixture = mixture * shrink + jnp.dot(
            spread, rows[:, HD:], preferred_element_type=jnp.float32
        )
        return raised, weight_sum, mixture

    _, weight_sum, mixture = lax.fori_loop(
        0, 4, decode_step, (own_score, jnp.ones((128, 1), jnp.float32), own_value)
    )
    mixed = (mixture / weight_sum).astype(jnp.bfloat16)
    for g in range(4):
        decode_out[:, pl.ds(g * HD, HD)] = mixed[g * count : (g + 1) * count]
    decoded = pltpu.make_async_copy(decode_out, decode_hbm, store_sem.at[0])
    decoded.start()

    steps = (1, 2, -1, -2)

    def bundle_copy(i):
        back = steps.index(-steps[i])
        return remote(bundle, near.at[back], bsend.at[back], brecv.at[back], device(0, steps[i]))

    def bundle_wait(i):
        return remote(bundle, near.at[i], bsend.at[i], brecv.at[i], device(0, steps[i]))

    bundle[...] = jnp.full((8, 128), -1, jnp.int32)
    for e in range(4):
        if e:
            table_copy(e).wait_recv()
        bundle[e : e + 1, :] = tabs[e, 0:1, :]
    for i in range(4):
        bundle_copy(i).start()
    moved = pltpu.make_async_copy(bundle, tabs_s, smem_sem.at[0])
    moved.start()
    moved.wait()

    def plane_of(p):
        return plane(-p if p < 5 else p - 4)

    def hand_copy(p, ch, e):
        return remote(
            stage.at[p if p < 3 else p - 2, ch, e],
            inbox.at[p, ch, e],
            psend.at[p, ch, e],
            precv.at[p, ch, e],
            device(e, 0),
        )

    def asked(rows_s, e, owner, rank):
        return jnp.clip(rows_s[e, owner * 2 + rank], 0, 15)

    def hand_out(p, ch):
        owner = yl * 16 + plane_of(p) * 2 + c
        for e in (3, 2, 1, 0):
            for rank in range(2):
                slot = asked(tabs_s, e, owner, rank)
                if p == 0:
                    first = pl.multiple_of(xh * HALF + ch * PIECE, PIECE)
                    rows = pool_v[slot, pl.ds(first, PIECE), :]
                else:
                    d, k = (0, p) if p < 5 else (1, p - 4)
                    rows = hop_bufs[d][k - 1][ch][slot]
                place = pl.ds(rank * PIECE, PIECE)
                if e == 0:
                    inbox[p, ch, 0, place, :] = rows
                else:
                    stage[p if p < 3 else p - 2, ch, e, place, :] = rows
            if e:
                hand_copy(p, ch, e).start()

    for ch in range(CHUNKS):
        hand_out(0, ch)

    def forward(ch):
        for d in range(2):
            ring(d, 1, ch).wait_recv()
            ring(d, 2, ch).start()

    forward(0)
    hand_out(1, 0)
    hand_out(5, 0)

    for copy in loads[7:]:
        copy.wait()
    fresh_keys = skv_ref[:, :HD]
    fresh_values = jnp.concatenate([skv_ref[:, HD:], jnp.ones((256, HD), jnp.bfloat16)], axis=1)
    causal = lax.broadcasted_iota(jnp.int32, (256, 256), 0) >= lax.broadcasted_iota(
        jnp.int32, (256, 256), 1
    )

    def fresh_step(h, carried):
        for i in range(2):
            rows = pl.ds(pl.multiple_of((2 * h + i) * 256, 256), 256)
            masked = jnp.where(causal, nt_dot(qall[rows, :], fresh_keys), LOW)
            highest = jnp.broadcast_to(jnp.max(masked, axis=1, keepdims=True), (256, HD))
            weights = jnp.concatenate(
                [
                    jnp.exp2((masked[:, j * HD : (j + 1) * HD] - highest) * SCALE)
                    for j in range(2)
                ],
                axis=1,
            )
            top[rows, :] = highest
            acc[rows, :] = jnp.dot(
                weights.astype(jnp.bfloat16), fresh_values, preferred_element_type=jnp.float32
            )
            rows = pl.ds(pl.multiple_of((4 + 2 * h + i) * 256, 256), 256)
            top[rows, :] = jnp.full((256, HD), LOW, jnp.float32)
            acc[rows, :] = jnp.zeros((256, 2 * HD), jnp.float32)
        return carried

    lax.fori_loop(0, 2, fresh_step, 0)
    forward(1)
    hand_out(1, 1)
    hand_out(5, 1)

    seen_key = jnp.broadcast_to(skv_ref[0:1, :HD].astype(jnp.float32), (PIECE, HD)).astype(
        jnp.bfloat16
    )

    def prepare(unit, place):
        for i, (p, ch) in enumerate(unit):
            for e in range(4):
                py, pc = peer(e)
                owner = py * 16 + plane_of(p) * 2 + pc
                for rank in range(2):
                    used = tabs_s[0, owner * 2 + rank] >= 0
                    cell = inbox[p, ch, e, pl.ds(rank * PIECE, PIECE), :]
                    rows = pl.ds(((i * 4 + e) * 2 + rank) * PIECE, PIECE)
                    keys[place, rows, :] = jnp.where(used, cell[:, :HD], seen_key)
                    values[place, rows, :HD] = jnp.where(
                        used, cell[:, HD:], jnp.zeros((PIECE, HD), jnp.bfloat16)
                    )
                    values[place, rows, HD:] = jnp.where(
                        used,
                        jnp.ones((PIECE, HD), jnp.bfloat16),
                        jnp.zeros((PIECE, HD), jnp.bfloat16),
                    )

    def whole(p):
        return [(p, ch) for ch in range(CHUNKS)]

    def tile_rows(tile):
        if isinstance(tile, int):
            return pl.ds(tile * TILE, TILE)
        return pl.ds(pl.multiple_of(tile * TILE, TILE), TILE)

    def score(place, tile, slot):
        scored[slot] = nt_dot(qall[tile_rows(tile), :], keys[place])

    def fold(place, tile, slot):
        rows = tile_rows(tile)
        parts = [scored[slot, :, j * HD : (j + 1) * HD] for j in range(4)]
        highest = top[rows, :]
        most = jnp.maximum(jnp.maximum(parts[0], parts[1]), jnp.maximum(parts[2], parts[3]))
        raised = jnp.maximum(
            highest, jnp.broadcast_to(jnp.max(most, axis=1, keepdims=True), (TILE, HD))
        )
        weights = jnp.concatenate(
            [jnp.exp2((part - raised) * SCALE).astype(jnp.bfloat16) for part in parts], axis=1
        )
        shrink = jnp.exp2((highest - raised) * SCALE)
        top[rows, :] = raised
        gained = jnp.dot(weights, values[place], preferred_element_type=jnp.float32)
        acc[rows, :HD] = acc[rows, :HD] * shrink + gained[:, :HD]
        acc[rows, HD:] = acc[rows, HD:] * shrink + gained[:, HD:]

    def attend(places):
        last = 4 * places - 1
        score(0, 0, 0)

        def two(j, carried):
            i = 2 * j
            score((i + 1) // 4, (i + 1) % 4, 1)
            fold(i // 4, i % 4, 0)
            after = jnp.minimum(i + 2, last)
            score(after // 4, after % 4, 0)
            fold((i + 1) // 4, (i + 1) % 4, 1)
            return carried

        lax.fori_loop(0, 2 * places, two, 0)

    both_chunks = tuple(range(CHUNKS))

    def collect(p, chunks):
        for ch in chunks:
            for e in range(1, 4):
                hand_copy(p, ch, e).wait_recv()

    for h in range(4):
        query_copy(h).wait_recv()
    collect(0, both_chunks)
    prepare(whole(0), 0)
    attend(1)

    for i in range(4):
        bundle_wait(i).wait_recv()
        moved = pltpu.make_async_copy(near.at[i], near_s.at[i], smem_sem.at[1 + i])
        moved.start()
        moved.wait()

    def near_copy(d, ch, e):
        return remote(
            near_stage.at[d, ch, e],
            inbox.at[(3, 7)[d], ch, e],
            nsend.at[d, ch, e],
            nrecv.at[d, ch, e],
            device(e, up_down[d]),
        )

    def far_copy(d, ch):
        return remote(
            far_stage.at[d, ch],
            far_in.at[d, ch],
            fsend.at[d, ch],
            frecv.at[d, ch],
            device(0, up_down[d]),
        )

    def last_copy(d, ch, e):
        return remote(
            far_in.at[d, ch, e],
            inbox.at[4, ch, e, pl.ds(d * PIECE, PIECE)],
            gsend.at[d, ch, e],
            grecv.at[d, ch, e],
            device(e, up_down[d]),
        )

    def send_far(ch):
        for d in range(2):
            ring(d, 2, ch).wait_recv()
            block = hop_bufs[d][1][ch]
            owner = yl * 16 + plane(-2 * up_down[d]) * 2 + c
            for e in range(4):
                far_stage[d, ch, e] = block[asked(near_s.at[2 * d + 1], e, owner, d)]
            far_copy(d, ch).start()

    def send_near(ch):
        for d in range(2):
            block = hop_bufs[d][1][ch]
            owner = yl * 16 + plane(-2 * up_down[d]) * 2 + c
            for e in (3, 2, 1, 0):
                for rank in range(2):
                    slot = asked(near_s.at[2 * d], e, owner, rank)
                    near_stage[d, ch, e, pl.ds(rank * PIECE, PIECE), :] = block[slot]
                near_copy(d, ch, e).start()

    send_far(0)
    send_near(0)
    hand_out(2, 0)
    hand_out(6, 0)
    for place, p in enumerate((1, 5)):
        collect(p, both_chunks)
        prepare(whole(p), place)
    attend(2)
    send_far(1)
    send_near(1)
    hand_out(2, 1)
    hand_out(6, 1)

    def forward_far(ch):
        for d in range(2):
            far_copy(d, ch).wait_recv()
            for e in (3, 2, 1, 0):
                last_copy(d, ch, e).start()

    def pair_unit(p, ch, theirs=False):
        unit = [(p, ch), (p + 4, ch)]
        if p < 3:
            for q, _ in unit:
                collect(q, (ch,))
        else:
            for d in range(2):
                for e in range(4):
                    near_copy(d, ch, e).wait_recv()
        prepare(unit, 0)
        if theirs:
            score(0, 2, 0)
            score(0, 3, 1)
            fold(0, 2, 0)
            fold(0, 3, 1)
        else:
            attend(1)

    forward_far(0)
    pair_unit(2, 0)
    forward_far(1)
    pair_unit(2, 1)
    pair_unit(3, 0)
    pair_unit(3, 1, True)
    for d, ch in both:
        for e in range(4):
            last_copy(d, ch, e).wait_recv()
    prepare(whole(4), 1)

    def part_copy(i):
        return remote(part_out.at[i], part_in.at[i], osend.at[i], orecv.at[i], xid)

    def stat_copy(i):
        return remote(stat_out.at[i], stat_in.at[i], ssend.at[i], srecv.at[i], xid)

    def hand_back(i):
        base = (2 + i) * TILE
        part_out[i] = acc[pl.ds(base, TILE), :HD].astype(jnp.bfloat16)
        part_copy(i).start()
        for j in range(4):
            rows = pl.ds(base + j * HD, HD)
            stat_out[i, j : j + 1, :] = as_row(top[rows, :])
            stat_out[i, 4 + j : 5 + j, :] = as_row(acc[rows, HD:])
        stat_copy(i).start()

    score(1, 2, 0)
    score(1, 3, 1)
    fold(1, 2, 0)
    hand_back(0)
    score(0, 0, 0)
    fold(1, 3, 1)
    hand_back(1)
    score(0, 1, 1)
    fold(0, 0, 0)
    score(1, 0, 0)
    fold(0, 1, 1)
    score(1, 1, 1)
    fold(1, 0, 0)
    fold(1, 1, 1)

    for d, ch in both:
        ring(d, 1, ch).wait_send()
        ring(d, 2, ch).wait_send()
        far_copy(d, ch).wait_send()
        for e in range(4):
            near_copy(d, ch, e).wait_send()
            last_copy(d, ch, e).wait_send()
    for i in range(4):
        bundle_copy(i).wait_send()
        query_copy(i).wait_send()
    for e in range(1, 4):
        table_copy(e).wait_send()
        for p in (0, 1, 2, 5, 6):
            for ch in range(CHUNKS):
                hand_copy(p, ch, e).wait_send()
    stored = [decoded]
    for i in range(2):
        part_copy(i).wait_recv()
        stat_copy(i).wait_recv()
        for j in range(4):
            base = i * TILE + j * HD
            rows = pl.ds(base, HD)
            here = top[rows, :]
            there = jnp.broadcast_to(column(stat_in[i, j : j + 1, :]), (HD, HD))
            extra = jnp.broadcast_to(column(stat_in[i, 4 + j : 5 + j, :]), (HD, HD))
            peak = jnp.maximum(here, there)
            keep, take = jnp.exp2((here - peak) * SCALE), jnp.exp2((there - peak) * SCALE)
            sums = acc[rows, HD:] * keep + extra * take
            mixed = acc[rows, :HD] * keep + part_in[i, pl.ds(j * HD, HD), :].astype(
                jnp.float32
            ) * take
            span_out[pl.ds(base % 256, HD), pl.ds(base // 256 * HD, HD)] = (mixed / sums).astype(
                jnp.bfloat16
            )
            if j % 2:
                h = 2 * i + j // 2
                stored.append(
                    pltpu.make_async_copy(
                        span_out.at[:, pl.ds(h * HD, HD)],
                        span_hbm.at[:, pl.ds(h * HD, HD)],
                        store_sem.at[1 + h],
                    )
                )
                stored[-1].start()

    for i in range(2):
        part_copy(i).wait_send()
        stat_copy(i).wait_send()
    for copy in stored:
        copy.wait()


def staged(*refs):
    first = 9 + 2 + 9 + 2
    flat = refs[first : first + 8]
    bufs = tuple(tuple(tuple(flat[(d * 2 + k) * 2 + ch] for ch in range(2)) for k in range(2)) for d in range(2))
    kernel(*refs[:first], bufs, *refs[first + 8 :])


def place_results(span_ref, decode_ref, span_out, decode_out):
    span_out[...] = span_ref[...]
    decode_out[...] = decode_ref[...]


def local(
    span_query,
    span_kv,
    kv_pool,
    hit_owner,
    hit_slot,
    decode_query,
    decode_kv,
    decode_table,
    decode_length,
):
    hbm = pl.BlockSpec(memory_space=pl.ANY)
    dma = pltpu.SemaphoreType.DMA
    bf16, f32 = jnp.bfloat16, jnp.float32
    results = pl.pallas_call(
        staged,
        out_shape=(
            jax.ShapeDtypeStruct(span_query.shape, bf16),
            jax.ShapeDtypeStruct(decode_query.shape, bf16),
        ),
        in_specs=[hbm] * 9,
        out_specs=(hbm, hbm),
        scratch_shapes=[
            pltpu.SMEM((32,), jnp.int32),
            pltpu.SMEM((32,), jnp.int32),
            pltpu.VMEM((4, 32), jnp.int32),
            pltpu.VMEM((1, 32), jnp.int32),
            pltpu.VMEM(decode_query.shape, bf16),
            pltpu.VMEM(decode_kv.shape, bf16),
            pltpu.VMEM(span_kv.shape, bf16),
            pltpu.VMEM(span_query.shape, bf16),
            pltpu.VMEM(decode_query.shape, bf16),
            pltpu.VMEM((16, 128, 256), bf16),
            pltpu.VMEM((2048, HD), bf16),
        ]
        + [pltpu.VMEM((16, PIECE, 256), bf16)] * 8
        + [
            pltpu.VMEM((5, CHUNKS, 4, 2 * PIECE, 256), bf16),
            pltpu.VMEM((2, CHUNKS, 4, 2 * PIECE, 256), bf16),
            pltpu.VMEM((2, CHUNKS, 4, PIECE, 256), bf16),
            pltpu.VMEM((2, CHUNKS, 4, PIECE, 256), bf16),
            pltpu.VMEM((NZ, CHUNKS, 4, 2 * PIECE, 256), bf16),
            pltpu.VMEM((4, 8, 128), jnp.int32),
            pltpu.SMEM((8, 128), jnp.int32),
            pltpu.VMEM((8, 128), jnp.int32),
            pltpu.VMEM((4, 8, 128), jnp.int32),
            pltpu.SMEM((4, 8, 128), jnp.int32),
            pltpu.VMEM((2, 512, HD), bf16),
            pltpu.VMEM((2, 512, 2 * HD), bf16),
            pltpu.VMEM((2, TILE, 512), f32),
            pltpu.VMEM((2048, 2 * HD), f32),
            pltpu.VMEM((2048, HD), f32),
            pltpu.VMEM((2, TILE, HD), bf16),
            pltpu.VMEM((2, TILE, HD), bf16),
            pltpu.VMEM((2, 8, 128), f32),
            pltpu.VMEM((2, 8, 128), f32),
            dma((12,)),
            dma((5,)),
            dma((2, 2, CHUNKS)),
            dma((2, 2, CHUNKS)),
            dma((NZ, CHUNKS, 4)),
            dma((NZ, CHUNKS, 4)),
            dma((2, CHUNKS, 4)),
            dma((2, CHUNKS, 4)),
            dma((2, CHUNKS)),
            dma((2, CHUNKS)),
            dma((2, CHUNKS, 4)),
            dma((2, CHUNKS, 4)),
            dma((4,)),
            dma((4,)),
            dma((4,)),
            dma((4,)),
            dma((5,)),
            dma((4,)),
            dma((4,)),
            dma((2,)),
            dma((2,)),
            dma((2,)),
            dma((2,)),
        ],
        compiler_params=pltpu.CompilerParams(
            collective_id=0, has_side_effects=True, vmem_limit_bytes=56 * 1024 * 1024
        ),
        cost_estimate=pl.CostEstimate(
            flops=5 * 10**9, bytes_accessed=3 * 2**20, transcendentals=10**7
        ),
        name="spanned_attention",
    )(
        hit_owner.reshape(-1),
        hit_slot,
        decode_table.T,
        decode_length,
        decode_query,
        decode_kv,
        span_kv,
        span_query,
        kv_pool,
    )
    vmem = pl.BlockSpec(memory_space=pltpu.VMEM)
    return pl.pallas_call(
        place_results,
        out_shape=(
            jax.ShapeDtypeStruct(span_query.shape, bf16),
            jax.ShapeDtypeStruct(decode_query.shape, bf16),
        ),
        in_specs=[vmem] * 2,
        out_specs=(vmem,) * 2,
        name="place_results",
    )(*results)


def solution(mesh):
    placed = (
        P("replica", "tensor"),
        P("replica", "tensor"),
        P("replica", None, "tensor"),
        P("replica", None),
        P("replica"),
        P("replica", "tensor"),
        P("replica", "tensor"),
        P("replica", None),
        P("replica", None),
    )
    return jax.shard_map(
        local,
        mesh=mesh,
        in_specs=placed,
        out_specs=(P("replica", "tensor"), P("replica", "tensor")),
        check_vma=False,
    )
```

```python
import functools
import math

import jax
import jax.numpy as jnp
from jax import lax
from jax.experimental import pallas as pl
from jax.experimental.pallas import tpu as pltpu
from jax.sharding import PartitionSpec as P

MESH = pl.DeviceIdType.MESH
HD = 128
NZ = 8
HALF = 64
CHUNKS = 2
PIECE = HALF // CHUNKS
TILE = 512
SCALE = HD ** (-0.5) * math.log2(math.e)
LOW = -1e30


def nt_dot(a, b):
    return lax.dot_general(a, b, (((1,), (1,)), ((), ())), preferred_element_type=jnp.float32)


def column(row):
    n = row.shape[1]
    eye = lax.broadcasted_iota(jnp.int32, (n, n), 0) == lax.broadcasted_iota(jnp.int32, (n, n), 1)
    return jnp.sum(jnp.where(eye, jnp.broadcast_to(row, (n, n)), 0.0), axis=1, keepdims=True)


def as_row(replicated):
    eye = lax.broadcasted_iota(jnp.int32, (128, 128), 0) == lax.broadcasted_iota(
        jnp.int32, (128, 128), 1
    )
    return jnp.sum(jnp.where(eye, replicated, 0.0), axis=0, keepdims=True)


def kernel(
    owner_hbm,
    slot_hbm,
    table_hbm,
    length_hbm,
    dq_hbm,
    dkv_hbm,
    skv_hbm,
    q_hbm,
    pool_hbm,
    span_hbm,
    decode_hbm,
    owner_s,
    slot_s,
    table_ref,
    length_ref,
    dq_ref,
    dkv_ref,
    skv_ref,
    span_out,
    decode_out,
    pool_v,
    qall,
    hop_bufs,
    stage,
    near_stage,
    wide_stage,
    wide_in,
    far_stage,
    far_in,
    inbox,
    tabs,
    tabs_s,
    bundle,
    near,
    near_s,
    keys,
    values,
    scored,
    acc,
    top,
    part_out,
    part_in,
    stat_out,
    stat_in,
    load_sem,
    store_sem,
    zsend,
    zrecv,
    psend,
    precv,
    nsend,
    nrecv,
    fsend,
    frecv,
    gsend,
    grecv,
    tsend,
    trecv,
    bsend,
    brecv,
    smem_sem,
    qsend,
    qrecv,
    osend,
    orecv,
    ssend,
    srecv,
):
    r = lax.axis_index("replica")
    t = lax.axis_index("tensor")
    yl, z, c = r // 16, (r // 2) % NZ, r % 2
    xh = t % 2
    tx = t + 1 - 2 * xh

    def plane(step):
        return (z + step + NZ) % NZ

    def peer(e):
        return (yl if e < 2 else 1 - yl), (c if e % 2 == 0 else 1 - c)

    def device(e, step):
        py, pc = peer(e)
        return (py * 16 + plane(step) * 2 + pc, t)

    xid = (r, tx)
    up_down = (1, -1)
    partners = [device(e, 0) for e in range(1, 4)] + [xid]
    partners += [device(e, step) for e in range(4) for step in (1, -1)]
    partners += [device(0, 2), device(0, -2)]

    barrier = pltpu.get_barrier_semaphore()
    for other in partners:
        pl.semaphore_signal(barrier, inc=1, device_id=other, device_id_type=MESH)

    pairs = [
        (owner_hbm, owner_s),
        (slot_hbm, slot_s),
        (pool_hbm, pool_v),
        (table_hbm, table_ref),
        (length_hbm, length_ref),
        (dq_hbm, dq_ref),
        (dkv_hbm, dkv_ref),
        (skv_hbm, skv_ref),
    ]
    for h in range(4):
        pairs.append((q_hbm.at[:, pl.ds(h * HD, HD)], qall.at[pl.ds(h * 256, 256)]))
    loads = [pltpu.make_async_copy(src, dst, load_sem.at[i]) for i, (src, dst) in enumerate(pairs)]

    def remote(src, dst, send, recv, where):
        return pltpu.make_async_remote_copy(
            src_ref=src,
            dst_ref=dst,
            send_sem=send,
            recv_sem=recv,
            device_id=where,
            device_id_type=MESH,
        )

    def ring(d, k, ch):
        if k == 1:
            first = pl.multiple_of(xh * HALF + ch * PIECE, PIECE)
            src = pool_hbm.at[:, pl.ds(first, PIECE), :]
        else:
            src = hop_bufs[d][0][ch]
        return remote(
            src,
            hop_bufs[d][k - 1][ch],
            zsend.at[d, k - 1, ch],
            zrecv.at[d, k - 1, ch],
            device(0, up_down[d]),
        )

    both = [(d, ch) for ch in range(CHUNKS) for d in range(2)]

    pl.semaphore_wait(barrier, len(partners))
    for d, ch in both:
        ring(d, 1, ch).start()
    for copy in loads:
        copy.start()

    def query_copy(h):
        return remote(
            q_hbm.at[:, pl.ds(h * HD, HD)],
            qall.at[pl.ds((4 + h) * 256, 256)],
            qsend.at[h],
            qrecv.at[h],
            xid,
        )

    for copy in loads[:2]:
        copy.wait()

    lane = lax.broadcasted_iota(jnp.int32, (8, 128), 1)
    lane_owner, lane_rank = lane // 2, lane % 2

    def note_hit(i, carried):
        table, seen = carried
        match = lane_owner == owner_s[i]
        table = jnp.where(match & (seen == lane_rank), slot_s[i], table)
        return table, seen + match.astype(jnp.int32)

    table, _ = lax.fori_loop(
        0,
        32,
        note_hit,
        (jnp.full((8, 128), -1, jnp.int32), jnp.zeros((8, 128), jnp.int32)),
    )
    tabs[0] = table

    def table_copy(e):
        return remote(tabs.at[0], tabs.at[e], tsend.at[e], trecv.at[e], device(e, 0))

    for e in range(1, 4):
        table_copy(e).start()
    for h in range(4):
        query_copy(h).start()

    for copy in loads[2:7]:
        copy.wait()
    count = 32
    dq = jnp.concatenate([dq_ref[:, pl.ds(g * HD, HD)] for g in range(4)], axis=0)
    lengths = column(length_ref[...].astype(jnp.float32))
    names = [column(table_ref[b : b + 1, :].astype(jnp.float32)) for b in range(4)]
    spot = lax.broadcasted_iota(jnp.int32, (count, HD), 1).astype(jnp.float32)

    def times(block):
        seen = jnp.zeros((count, HD), jnp.float32)
        for b in range(4):
            limit = jnp.where(names[b] == block, lengths - 128.0 * b, 0.0)
            seen = seen + jnp.where(spot < limit, 1.0, 0.0)
        return jnp.concatenate([seen] * 4, axis=0)

    own_key = jnp.concatenate([dkv_ref[:, :HD].astype(jnp.float32)] * 4, axis=0)
    own_value = jnp.concatenate([dkv_ref[:, HD:].astype(jnp.float32)] * 4, axis=0)
    own_score = jnp.sum(dq.astype(jnp.float32) * own_key, axis=1, keepdims=True)

    def decode_step(it, carried):
        highest, weight_sum, mixture = carried
        rows = pool_v[pl.ds(it * 4, 4)].reshape(4 * HD, 2 * HD)
        scores = nt_dot(dq, rows[:, :HD])
        seen = jnp.concatenate([times((it * 4 + i).astype(jnp.float32)) for i in range(4)], axis=1)
        masked = jnp.where(seen > 0.0, scores, LOW)
        raised = jnp.maximum(highest, jnp.max(masked, axis=1, keepdims=True))
        weights = jnp.exp2((masked - raised) * SCALE)
        shrink = jnp.exp2((highest - raised) * SCALE)
        weight_sum = weight_sum * shrink + jnp.sum(weights * seen, axis=1, keepdims=True)
        spread = (weights.astype(jnp.bfloat16).astype(jnp.float32) * seen).astype(jnp.bfloat16)
        mixture = mixture * shrink + jnp.dot(
            spread, rows[:, HD:], preferred_element_type=jnp.float32
        )
        return raised, weight_sum, mixture

    _, weight_sum, mixture = lax.fori_loop(
        0, 4, decode_step, (own_score, jnp.ones((128, 1), jnp.float32), own_value)
    )
    mixed = (mixture / weight_sum).astype(jnp.bfloat16)
    for g in range(4):
        decode_out[:, pl.ds(g * HD, HD)] = mixed[g * count : (g + 1) * count]
    decoded = pltpu.make_async_copy(decode_out, decode_hbm, store_sem.at[0])
    decoded.start()

    steps = (1, 2, -1, -2)

    def bundle_copy(i):
        back = steps.index(-steps[i])
        return remote(bundle, near.at[back], bsend.at[back], brecv.at[back], device(0, steps[i]))

    def bundle_wait(i):
        return remote(bundle, near.at[i], bsend.at[i], brecv.at[i], device(0, steps[i]))

    bundle[...] = jnp.full((8, 128), -1, jnp.int32)
    for e in range(4):
        if e:
            table_copy(e).wait_recv()
        bundle[e : e + 1, :] = tabs[e, 0:1, :]
    for i in range(4):
        bundle_copy(i).start()
    moved = pltpu.make_async_copy(bundle, tabs_s, smem_sem.at[0])
    moved.start()
    moved.wait()

    def plane_of(p):
        return plane(-p if p < 5 else p - 4)

    def hand_copy(p, ch, e):
        return remote(
            stage.at[p if p < 3 else p - 2, ch, e],
            inbox.at[p, ch, e],
            psend.at[p, ch, e],
            precv.at[p, ch, e],
            device(e, 0),
        )

    def asked(rows_s, e, owner, rank):
        return jnp.clip(rows_s[e, owner * 2 + rank], 0, 15)

    def hand_out(p, ch):
        owner = yl * 16 + plane_of(p) * 2 + c
        for e in (3, 2, 1, 0):
            for rank in range(2):
                slot = asked(tabs_s, e, owner, rank)
                if p == 0:
                    first = pl.multiple_of(xh * HALF + ch * PIECE, PIECE)
                    rows = pool_v[slot, pl.ds(first, PIECE), :]
                else:
                    d, k = (0, p) if p < 5 else (1, p - 4)
                    rows = hop_bufs[d][k - 1][ch][slot]
                place = pl.ds(rank * PIECE, PIECE)
                if e == 0:
                    inbox[p, ch, 0, place, :] = rows
                else:
                    stage[p if p < 3 else p - 2, ch, e, place, :] = rows
            if e:
                hand_copy(p, ch, e).start()

    for ch in range(CHUNKS):
        hand_out(0, ch)

    def forward(ch):
        for d in range(2):
            ring(d, 1, ch).wait_recv()
            ring(d, 2, ch).start()

    forward(0)
    hand_out(1, 0)
    hand_out(5, 0)

    for copy in loads[7:]:
        copy.wait()
    fresh_keys = skv_ref[:, :HD]
    fresh_values = jnp.concatenate([skv_ref[:, HD:], jnp.ones((256, HD), jnp.bfloat16)], axis=1)
    causal = lax.broadcasted_iota(jnp.int32, (256, 256), 0) >= lax.broadcasted_iota(
        jnp.int32, (256, 256), 1
    )

    def fresh_step(h, carried):
        for i in range(2):
            rows = pl.ds(pl.multiple_of((2 * h + i) * 256, 256), 256)
            masked = jnp.where(causal, nt_dot(qall[rows, :], fresh_keys), LOW)
            highest = jnp.broadcast_to(jnp.max(masked, axis=1, keepdims=True), (256, HD))
            weights = jnp.concatenate(
                [
                    jnp.exp2((masked[:, j * HD : (j + 1) * HD] - highest) * SCALE)
                    for j in range(2)
                ],
                axis=1,
            )
            top[rows, :] = highest
            acc[rows, :] = jnp.dot(
                weights.astype(jnp.bfloat16), fresh_values, preferred_element_type=jnp.float32
            )
            rows = pl.ds(pl.multiple_of((4 + 2 * h + i) * 256, 256), 256)
            top[rows, :] = jnp.full((256, HD), LOW, jnp.float32)
            acc[rows, :] = jnp.zeros((256, 2 * HD), jnp.float32)
        return carried

    lax.fori_loop(0, 2, fresh_step, 0)
    forward(1)
    hand_out(1, 1)
    hand_out(5, 1)

    seen_key = jnp.broadcast_to(skv_ref[0:1, :HD].astype(jnp.float32), (PIECE, HD)).astype(
        jnp.bfloat16
    )

    def prepare(unit, place):
        for i, (p, ch) in enumerate(unit):
            for e in range(4):
                py, pc = peer(e)
                owner = py * 16 + plane_of(p) * 2 + pc
                for rank in range(2):
                    used = tabs_s[0, owner * 2 + rank] >= 0
                    cell = inbox[p, ch, e, pl.ds(rank * PIECE, PIECE), :]
                    rows = pl.ds(((i * 4 + e) * 2 + rank) * PIECE, PIECE)
                    keys[place, rows, :] = jnp.where(used, cell[:, :HD], seen_key)
                    values[place, rows, :HD] = jnp.where(
                        used, cell[:, HD:], jnp.zeros((PIECE, HD), jnp.bfloat16)
                    )
                    values[place, rows, HD:] = jnp.where(
                        used,
                        jnp.ones((PIECE, HD), jnp.bfloat16),
                        jnp.zeros((PIECE, HD), jnp.bfloat16),
                    )

    def whole(p):
        return [(p, ch) for ch in range(CHUNKS)]

    def tile_rows(tile):
        if isinstance(tile, int):
            return pl.ds(tile * TILE, TILE)
        return pl.ds(pl.multiple_of(tile * TILE, TILE), TILE)

    def score(place, tile, slot):
        scored[slot] = nt_dot(qall[tile_rows(tile), :], keys[place])

    def fold(place, tile, slot):
        rows = tile_rows(tile)
        parts = [scored[slot, :, j * HD : (j + 1) * HD] for j in range(4)]
        highest = top[rows, :]
        most = jnp.maximum(jnp.maximum(parts[0], parts[1]), jnp.maximum(parts[2], parts[3]))
        raised = jnp.maximum(
            highest, jnp.broadcast_to(jnp.max(most, axis=1, keepdims=True), (TILE, HD))
        )
        weights = jnp.concatenate(
            [jnp.exp2((part - raised) * SCALE).astype(jnp.bfloat16) for part in parts], axis=1
        )
        shrink = jnp.exp2((highest - raised) * SCALE)
        top[rows, :] = raised
        gained = jnp.dot(weights, values[place], preferred_element_type=jnp.float32)
        acc[rows, :HD] = acc[rows, :HD] * shrink + gained[:, :HD]
        acc[rows, HD:] = acc[rows, HD:] * shrink + gained[:, HD:]

    def attend(places):
        last = 4 * places - 1
        score(0, 0, 0)

        def two(j, carried):
            i = 2 * j
            score((i + 1) // 4, (i + 1) % 4, 1)
            fold(i // 4, i % 4, 0)
            after = jnp.minimum(i + 2, last)
            score(after // 4, after % 4, 0)
            fold((i + 1) // 4, (i + 1) % 4, 1)
            return carried

        lax.fori_loop(0, 2 * places, two, 0)

    both_chunks = tuple(range(CHUNKS))

    def collect(p, chunks):
        for ch in chunks:
            for e in range(1, 4):
                hand_copy(p, ch, e).wait_recv()

    for h in range(4):
        query_copy(h).wait_recv()
    collect(0, both_chunks)
    prepare(whole(0), 0)
    attend(1)

    for i in range(4):
        bundle_wait(i).wait_recv()
        moved = pltpu.make_async_copy(near.at[i], near_s.at[i], smem_sem.at[1 + i])
        moved.start()
        moved.wait()

    def near_copy(d, ch, e):
        return remote(
            near_stage.at[d, ch, e],
            inbox.at[(3, 7)[d], ch, e],
            nsend.at[d, ch, e],
            nrecv.at[d, ch, e],
            device(e, up_down[d]),
        )

    def far_copy(d, ch):
        return remote(
            (wide_stage, far_stage)[ch].at[d],
            (wide_in, far_in)[ch].at[d],
            fsend.at[d, ch],
            frecv.at[d, ch],
            device(0, up_down[d]),
        )

    def last_copy(d, ch, e):
        place = inbox.at[4, ch, e] if ch == 0 else inbox.at[4, ch, e, pl.ds(d * PIECE, PIECE)]
        return remote(
            (wide_in, far_in)[ch].at[d, e],
            place,
            gsend.at[d, ch, e],
            grecv.at[d, ch, e],
            device(e, up_down[d]),
        )

    def on_way(d, hops):
        first = (z - hops * up_down[d] + NZ) % NZ
        return (first < 4) if d == 0 else (first >= 4)

    def if_used(d, ch, hops, do):
        if ch == 0:
            pl.when(on_way(d, hops))(do)
        else:
            do()

    def send_far(ch):
        for d in range(2):
            ring(d, 2, ch).wait_recv()
            block = hop_bufs[d][1][ch]
            owner = yl * 16 + plane(-2 * up_down[d]) * 2 + c

            def send(d=d, block=block, owner=owner):
                for e in range(4):
                    if ch == 0:
                        for rank in range(2):
                            slot = asked(near_s.at[2 * d + 1], e, owner, rank)
                            wide_stage[d, e, pl.ds(rank * PIECE, PIECE), :] = block[slot]
                    else:
                        far_stage[d, e] = block[asked(near_s.at[2 * d + 1], e, owner, d)]
                far_copy(d, ch).start()

            if_used(d, ch, 2, send)

    def send_near(ch):
        for d in range(2):
            block = hop_bufs[d][1][ch]
            owner = yl * 16 + plane(-2 * up_down[d]) * 2 + c
            for e in (3, 2, 1, 0):
                for rank in range(2):
                    slot = asked(near_s.at[2 * d], e, owner, rank)
                    near_stage[d, ch, e, pl.ds(rank * PIECE, PIECE), :] = block[slot]
                near_copy(d, ch, e).start()

    def forward_far(ch):
        for d in range(2):

            def pass_on(d=d):
                far_copy(d, ch).wait_recv()
                for e in (3, 2, 1, 0):
                    last_copy(d, ch, e).start()

            if_used(d, ch, 3, pass_on)

    def pair_unit(p, ch, theirs=False):
        unit = [(p, ch), (p + 4, ch)]
        if p < 3:
            for q, _ in unit:
                collect(q, (ch,))
        else:
            for d in range(2):
                for e in range(4):
                    near_copy(d, ch, e).wait_recv()
        prepare(unit, 0)
        if theirs:
            score(0, 2, 0)
            score(0, 3, 1)
            fold(0, 2, 0)
            fold(0, 3, 1)
        else:
            attend(1)

    pair_unit(1, 0)
    send_far(0)
    send_near(0)
    hand_out(2, 0)
    hand_out(6, 0)
    send_far(1)
    send_near(1)
    hand_out(2, 1)
    hand_out(6, 1)
    pair_unit(1, 1)
    forward_far(0)
    pair_unit(2, 0)
    forward_far(1)
    pair_unit(2, 1)
    pair_unit(3, 0)
    pair_unit(3, 1, True)
    for d, ch in both:

        def arrive(d=d, ch=ch):
            for e in range(4):
                last_copy(d, ch, e).wait_recv()

        if_used(d, ch, 4, arrive)
    prepare(whole(4), 1)

    def part_copy(i):
        return remote(part_out.at[i], part_in.at[i], osend.at[i], orecv.at[i], xid)

    def stat_copy():
        return remote(stat_out, stat_in, ssend.at[0], srecv.at[0], xid)

    def send_part(i):
        part_out[i] = acc[pl.ds((2 + i) * TILE, TILE), :HD].astype(jnp.bfloat16)
        part_copy(i).start()

    def send_stats():
        for i in range(2):
            for j in range(4):
                rows = pl.ds((2 + i) * TILE + j * HD, HD)
                stat_out[i, j : j + 1, :] = as_row(top[rows, :])
                stat_out[i, 4 + j : 5 + j, :] = as_row(acc[rows, HD:])
        stat_copy().start()

    score(1, 2, 0)
    score(1, 3, 1)
    fold(1, 2, 0)
    send_part(0)
    score(0, 0, 0)
    fold(1, 3, 1)
    send_stats()
    send_part(1)
    score(0, 1, 1)
    fold(0, 0, 0)
    score(1, 0, 0)
    fold(0, 1, 1)
    score(1, 1, 1)
    fold(1, 0, 0)
    fold(1, 1, 1)

    for d, ch in both:
        ring(d, 1, ch).wait_send()
        ring(d, 2, ch).wait_send()
        for e in range(4):
            near_copy(d, ch, e).wait_send()

        def sent(d=d, ch=ch):
            far_copy(d, ch).wait_send()

        def passed(d=d, ch=ch):
            for e in range(4):
                last_copy(d, ch, e).wait_send()

        if_used(d, ch, 2, sent)
        if_used(d, ch, 3, passed)
    for i in range(4):
        bundle_copy(i).wait_send()
        query_copy(i).wait_send()
    for e in range(1, 4):
        table_copy(e).wait_send()
        for p in (0, 1, 2, 5, 6):
            for ch in range(CHUNKS):
                hand_copy(p, ch, e).wait_send()
    stored = [decoded]
    stat_copy().wait_recv()
    for i in range(2):
        for j in range(4):
            rows = pl.ds(i * TILE + j * HD, HD)
            here = top[rows, :]
            there = jnp.broadcast_to(column(stat_in[i, j : j + 1, :]), (HD, HD))
            extra = jnp.broadcast_to(column(stat_in[i, 4 + j : 5 + j, :]), (HD, HD))
            peak = jnp.maximum(here, there)
            keep, take = jnp.exp2((here - peak) * SCALE), jnp.exp2((there - peak) * SCALE)
            inverse = 1.0 / (acc[rows, HD:] * keep + extra * take)
            acc[rows, :HD] = acc[rows, :HD] * (keep * inverse)
            top[rows, :] = take * inverse
    for h in range(4):
        if h % 2 == 0:
            part_copy(h // 2).wait_recv()
        rows = pl.ds(h * 256, 256)
        other = part_in[h // 2, pl.ds(h % 2 * 256, 256), :].astype(jnp.float32)
        span_out[:, pl.ds(h * HD, HD)] = (acc[rows, :HD] + other * top[rows, :]).astype(
            jnp.bfloat16
        )
        stored.append(
            pltpu.make_async_copy(
                span_out.at[:, pl.ds(h * HD, HD)],
                span_hbm.at[:, pl.ds(h * HD, HD)],
                store_sem.at[1 + h],
            )
        )
        stored[-1].start()

    for i in range(2):
        part_copy(i).wait_send()
    stat_copy().wait_send()
    for copy in stored:
        copy.wait()


def staged(*refs):
    first = 9 + 2 + 9 + 2
    flat = refs[first : first + 8]
    bufs = tuple(tuple(tuple(flat[(d * 2 + k) * 2 + ch] for ch in range(2)) for k in range(2)) for d in range(2))
    kernel(*refs[:first], bufs, *refs[first + 8 :])


def place_results(span_ref, decode_ref, span_out, decode_out):
    span_out[...] = span_ref[...]
    decode_out[...] = decode_ref[...]


def local(
    span_query,
    span_kv,
    kv_pool,
    hit_owner,
    hit_slot,
    decode_query,
    decode_kv,
    decode_table,
    decode_length,
):
    hbm = pl.BlockSpec(memory_space=pl.ANY)
    dma = pltpu.SemaphoreType.DMA
    bf16, f32 = jnp.bfloat16, jnp.float32
    results = pl.pallas_call(
        staged,
        out_shape=(
            jax.ShapeDtypeStruct(span_query.shape, bf16),
            jax.ShapeDtypeStruct(decode_query.shape, bf16),
        ),
        in_specs=[hbm] * 9,
        out_specs=(hbm, hbm),
        scratch_shapes=[
            pltpu.SMEM((32,), jnp.int32),
            pltpu.SMEM((32,), jnp.int32),
            pltpu.VMEM((4, 32), jnp.int32),
            pltpu.VMEM((1, 32), jnp.int32),
            pltpu.VMEM(decode_query.shape, bf16),
            pltpu.VMEM(decode_kv.shape, bf16),
            pltpu.VMEM(span_kv.shape, bf16),
            pltpu.VMEM(span_query.shape, bf16),
            pltpu.VMEM(decode_query.shape, bf16),
            pltpu.VMEM((16, 128, 256), bf16),
            pltpu.VMEM((2048, HD), bf16),
        ]
        + [pltpu.VMEM((16, PIECE, 256), bf16)] * 8
        + [
            pltpu.VMEM((5, CHUNKS, 4, 2 * PIECE, 256), bf16),
            pltpu.VMEM((2, CHUNKS, 4, 2 * PIECE, 256), bf16),
            pltpu.VMEM((2, 4, 2 * PIECE, 256), bf16),
            pltpu.VMEM((2, 4, 2 * PIECE, 256), bf16),
            pltpu.VMEM((2, 4, PIECE, 256), bf16),
            pltpu.VMEM((2, 4, PIECE, 256), bf16),
            pltpu.VMEM((NZ, CHUNKS, 4, 2 * PIECE, 256), bf16),
            pltpu.VMEM((4, 8, 128), jnp.int32),
            pltpu.SMEM((8, 128), jnp.int32),
            pltpu.VMEM((8, 128), jnp.int32),
            pltpu.VMEM((4, 8, 128), jnp.int32),
            pltpu.SMEM((4, 8, 128), jnp.int32),
            pltpu.VMEM((2, 512, HD), bf16),
            pltpu.VMEM((2, 512, 2 * HD), bf16),
            pltpu.VMEM((2, TILE, 512), f32),
            pltpu.VMEM((2048, 2 * HD), f32),
            pltpu.VMEM((2048, HD), f32),
            pltpu.VMEM((2, TILE, HD), bf16),
            pltpu.VMEM((2, TILE, HD), bf16),
            pltpu.VMEM((2, 8, 128), f32),
            pltpu.VMEM((2, 8, 128), f32),
            dma((12,)),
            dma((5,)),
            dma((2, 2, CHUNKS)),
            dma((2, 2, CHUNKS)),
            dma((NZ, CHUNKS, 4)),
            dma((NZ, CHUNKS, 4)),
            dma((2, CHUNKS, 4)),
            dma((2, CHUNKS, 4)),
            dma((2, CHUNKS)),
            dma((2, CHUNKS)),
            dma((2, CHUNKS, 4)),
            dma((2, CHUNKS, 4)),
            dma((4,)),
            dma((4,)),
            dma((4,)),
            dma((4,)),
            dma((5,)),
            dma((4,)),
            dma((4,)),
            dma((2,)),
            dma((2,)),
            dma((1,)),
            dma((1,)),
        ],
        compiler_params=pltpu.CompilerParams(
            collective_id=0, has_side_effects=True, vmem_limit_bytes=56 * 1024 * 1024
        ),
        cost_estimate=pl.CostEstimate(
            flops=5 * 10**9, bytes_accessed=3 * 2**20, transcendentals=10**7
        ),
        name="spanned_attention",
    )(
        hit_owner.reshape(-1),
        hit_slot,
        decode_table.T,
        decode_length,
        decode_query,
        decode_kv,
        span_kv,
        span_query,
        kv_pool,
    )
    vmem = pl.BlockSpec(memory_space=pltpu.VMEM)
    return pl.pallas_call(
        place_results,
        out_shape=(
            jax.ShapeDtypeStruct(span_query.shape, bf16),
            jax.ShapeDtypeStruct(decode_query.shape, bf16),
        ),
        in_specs=[vmem] * 2,
        out_specs=(vmem,) * 2,
        name="place_results",
    )(*results)


def solution(mesh):
    placed = (
        P("replica", "tensor"),
        P("replica", "tensor"),
        P("replica", None, "tensor"),
        P("replica", None),
        P("replica"),
        P("replica", "tensor"),
        P("replica", "tensor"),
        P("replica", None),
        P("replica", None),
    )
    return jax.shard_map(
        local,
        mesh=mesh,
        in_specs=placed,
        out_specs=(P("replica", "tensor"), P("replica", "tensor")),
        check_vma=False,
    )
```

```python
import functools
import math

import jax
import jax.numpy as jnp
from jax import lax
from jax.experimental import pallas as pl
from jax.experimental.pallas import tpu as pltpu
from jax.sharding import PartitionSpec as P

MESH = pl.DeviceIdType.MESH
HD = 128
NZ = 8
HALF = 64
CHUNKS = 2
PIECE = HALF // CHUNKS
TILE = 512
SCALE = HD ** (-0.5) * math.log2(math.e)
LOW = -1e30


def nt_dot(a, b):
    return lax.dot_general(a, b, (((1,), (1,)), ((), ())), preferred_element_type=jnp.float32)


def column(row):
    n = row.shape[1]
    eye = lax.broadcasted_iota(jnp.int32, (n, n), 0) == lax.broadcasted_iota(jnp.int32, (n, n), 1)
    return jnp.sum(jnp.where(eye, jnp.broadcast_to(row, (n, n)), 0.0), axis=1, keepdims=True)


def as_row(replicated):
    eye = lax.broadcasted_iota(jnp.int32, (128, 128), 0) == lax.broadcasted_iota(
        jnp.int32, (128, 128), 1
    )
    return jnp.sum(jnp.where(eye, replicated, 0.0), axis=0, keepdims=True)


def kernel(
    owner_hbm,
    slot_hbm,
    table_hbm,
    length_hbm,
    dq_hbm,
    dkv_hbm,
    skv_hbm,
    q_hbm,
    pool_hbm,
    span_hbm,
    decode_hbm,
    owner_s,
    slot_s,
    table_ref,
    length_ref,
    dq_ref,
    dkv_ref,
    skv_ref,
    span_out,
    decode_out,
    pool_v,
    qall,
    hop_bufs,
    stage,
    near_stage,
    wide_stage,
    wide_in,
    inbox,
    tabs,
    tabs_s,
    bundle,
    near,
    near_s,
    keys,
    values,
    scored,
    acc,
    top,
    part_out,
    part_in,
    stat_out,
    stat_in,
    load_sem,
    store_sem,
    zsend,
    zrecv,
    psend,
    precv,
    nsend,
    nrecv,
    fsend,
    frecv,
    gsend,
    grecv,
    tsend,
    trecv,
    bsend,
    brecv,
    smem_sem,
    qsend,
    qrecv,
    osend,
    orecv,
    ssend,
    srecv,
):
    r = lax.axis_index("replica")
    t = lax.axis_index("tensor")
    yl, z, c = r // 16, (r // 2) % NZ, r % 2
    xh = t % 2
    tx = t + 1 - 2 * xh

    def plane(step):
        return (z + step + NZ) % NZ

    def peer(e):
        return (yl if e < 2 else 1 - yl), (c if e % 2 == 0 else 1 - c)

    def device(e, step):
        py, pc = peer(e)
        return (py * 16 + plane(step) * 2 + pc, t)

    xid = (r, tx)
    up_down = (1, -1)
    partners = [device(e, 0) for e in range(1, 4)] + [xid]
    partners += [device(e, step) for e in range(4) for step in (1, -1)]
    partners += [device(0, 2), device(0, -2)]

    barrier = pltpu.get_barrier_semaphore()
    for other in partners:
        pl.semaphore_signal(barrier, inc=1, device_id=other, device_id_type=MESH)

    pairs = [
        (owner_hbm, owner_s),
        (slot_hbm, slot_s),
        (pool_hbm, pool_v),
        (table_hbm, table_ref),
        (length_hbm, length_ref),
        (dq_hbm, dq_ref),
        (dkv_hbm, dkv_ref),
        (skv_hbm, skv_ref),
    ]
    for h in range(4):
        pairs.append((q_hbm.at[:, pl.ds(h * HD, HD)], qall.at[pl.ds(h * 256, 256)]))
    loads = [pltpu.make_async_copy(src, dst, load_sem.at[i]) for i, (src, dst) in enumerate(pairs)]

    def remote(src, dst, send, recv, where):
        return pltpu.make_async_remote_copy(
            src_ref=src,
            dst_ref=dst,
            send_sem=send,
            recv_sem=recv,
            device_id=where,
            device_id_type=MESH,
        )

    def ring(d, k, ch):
        if k == 1:
            first = pl.multiple_of(xh * HALF + ch * PIECE, PIECE)
            src = pool_hbm.at[:, pl.ds(first, PIECE), :]
        else:
            src = hop_bufs[d][0][ch]
        return remote(
            src,
            hop_bufs[d][k - 1][ch],
            zsend.at[d, k - 1, ch],
            zrecv.at[d, k - 1, ch],
            device(0, up_down[d]),
        )

    both = [(d, ch) for ch in range(CHUNKS) for d in range(2)]

    pl.semaphore_wait(barrier, len(partners))
    for d, ch in both:
        ring(d, 1, ch).start()
    for copy in loads:
        copy.start()

    def query_copy(h):
        return remote(
            q_hbm.at[:, pl.ds(h * HD, HD)],
            qall.at[pl.ds((4 + h) * 256, 256)],
            qsend.at[h],
            qrecv.at[h],
            xid,
        )

    for copy in loads[:2]:
        copy.wait()

    lane = lax.broadcasted_iota(jnp.int32, (8, 128), 1)
    lane_owner, lane_rank = lane // 2, lane % 2

    def note_hit(i, carried):
        table, seen = carried
        match = lane_owner == owner_s[i]
        table = jnp.where(match & (seen == lane_rank), slot_s[i], table)
        return table, seen + match.astype(jnp.int32)

    table, _ = lax.fori_loop(
        0,
        32,
        note_hit,
        (jnp.full((8, 128), -1, jnp.int32), jnp.zeros((8, 128), jnp.int32)),
    )
    tabs[0] = table

    def table_copy(e):
        return remote(tabs.at[0], tabs.at[e], tsend.at[e], trecv.at[e], device(e, 0))

    for e in range(1, 4):
        table_copy(e).start()
    for h in range(4):
        query_copy(h).start()

    for copy in loads[2:7]:
        copy.wait()
    count = 32
    dq = jnp.concatenate([dq_ref[:, pl.ds(g * HD, HD)] for g in range(4)], axis=0)
    lengths = column(length_ref[...].astype(jnp.float32))
    names = [column(table_ref[b : b + 1, :].astype(jnp.float32)) for b in range(4)]
    spot = lax.broadcasted_iota(jnp.int32, (count, HD), 1).astype(jnp.float32)

    def times(block):
        seen = jnp.zeros((count, HD), jnp.float32)
        for b in range(4):
            limit = jnp.where(names[b] == block, lengths - 128.0 * b, 0.0)
            seen = seen + jnp.where(spot < limit, 1.0, 0.0)
        return jnp.concatenate([seen] * 4, axis=0)

    own_key = jnp.concatenate([dkv_ref[:, :HD].astype(jnp.float32)] * 4, axis=0)
    own_value = jnp.concatenate([dkv_ref[:, HD:].astype(jnp.float32)] * 4, axis=0)
    own_score = jnp.sum(dq.astype(jnp.float32) * own_key, axis=1, keepdims=True)

    def decode_step(it, carried):
        highest, weight_sum, mixture = carried
        rows = pool_v[pl.ds(it * 4, 4)].reshape(4 * HD, 2 * HD)
        scores = nt_dot(dq, rows[:, :HD])
        seen = jnp.concatenate([times((it * 4 + i).astype(jnp.float32)) for i in range(4)], axis=1)
        masked = jnp.where(seen > 0.0, scores, LOW)
        raised = jnp.maximum(highest, jnp.max(masked, axis=1, keepdims=True))
        weights = jnp.exp2((masked - raised) * SCALE)
        shrink = jnp.exp2((highest - raised) * SCALE)
        weight_sum = weight_sum * shrink + jnp.sum(weights * seen, axis=1, keepdims=True)
        spread = (weights.astype(jnp.bfloat16).astype(jnp.float32) * seen).astype(jnp.bfloat16)
        mixture = mixture * shrink + jnp.dot(
            spread, rows[:, HD:], preferred_element_type=jnp.float32
        )
        return raised, weight_sum, mixture

    _, weight_sum, mixture = lax.fori_loop(
        0, 4, decode_step, (own_score, jnp.ones((128, 1), jnp.float32), own_value)
    )
    mixed = (mixture / weight_sum).astype(jnp.bfloat16)
    for g in range(4):
        decode_out[:, pl.ds(g * HD, HD)] = mixed[g * count : (g + 1) * count]
    decoded = pltpu.make_async_copy(decode_out, decode_hbm, store_sem.at[0])
    decoded.start()

    steps = (1, 2, -1, -2)

    def bundle_copy(i):
        back = steps.index(-steps[i])
        return remote(bundle, near.at[back], bsend.at[back], brecv.at[back], device(0, steps[i]))

    def bundle_wait(i):
        return remote(bundle, near.at[i], bsend.at[i], brecv.at[i], device(0, steps[i]))

    bundle[...] = jnp.full((8, 128), -1, jnp.int32)
    for e in range(4):
        if e:
            table_copy(e).wait_recv()
        bundle[e : e + 1, :] = tabs[e, 0:1, :]
    for i in range(4):
        bundle_copy(i).start()
    moved = pltpu.make_async_copy(bundle, tabs_s, smem_sem.at[0])
    moved.start()
    moved.wait()

    def plane_of(p):
        return plane(-p if p < 5 else p - 4)

    def hand_copy(p, ch, e):
        return remote(
            stage.at[p if p < 3 else p - 2, ch, e],
            inbox.at[p, ch, e],
            psend.at[p, ch, e],
            precv.at[p, ch, e],
            device(e, 0),
        )

    def asked(rows_s, e, owner, rank):
        return jnp.clip(rows_s[e, owner * 2 + rank], 0, 15)

    def hand_out(p, ch):
        owner = yl * 16 + plane_of(p) * 2 + c
        for e in (3, 2, 1, 0):
            for rank in range(2):
                slot = asked(tabs_s, e, owner, rank)
                if p == 0:
                    first = pl.multiple_of(xh * HALF + ch * PIECE, PIECE)
                    rows = pool_v[slot, pl.ds(first, PIECE), :]
                else:
                    d, k = (0, p) if p < 5 else (1, p - 4)
                    rows = hop_bufs[d][k - 1][ch][slot]
                place = pl.ds(rank * PIECE, PIECE)
                if e == 0:
                    inbox[p, ch, 0, place, :] = rows
                else:
                    stage[p if p < 3 else p - 2, ch, e, place, :] = rows
            if e:
                hand_copy(p, ch, e).start()

    for ch in range(CHUNKS):
        hand_out(0, ch)

    def forward(ch):
        for d in range(2):
            ring(d, 1, ch).wait_recv()
            ring(d, 2, ch).start()

    forward(0)
    hand_out(1, 0)
    hand_out(5, 0)

    for copy in loads[7:]:
        copy.wait()
    fresh_keys = skv_ref[:, :HD]
    fresh_values = jnp.concatenate([skv_ref[:, HD:], jnp.ones((256, HD), jnp.bfloat16)], axis=1)
    causal = lax.broadcasted_iota(jnp.int32, (256, 256), 0) >= lax.broadcasted_iota(
        jnp.int32, (256, 256), 1
    )

    def fresh_step(h, carried):
        for i in range(2):
            rows = pl.ds(pl.multiple_of((2 * h + i) * 256, 256), 256)
            masked = jnp.where(causal, nt_dot(qall[rows, :], fresh_keys), LOW)
            highest = jnp.broadcast_to(jnp.max(masked, axis=1, keepdims=True), (256, HD))
            weights = jnp.concatenate(
                [
                    jnp.exp2((masked[:, j * HD : (j + 1) * HD] - highest) * SCALE)
                    for j in range(2)
                ],
                axis=1,
            )
            top[rows, :] = highest
            acc[rows, :] = jnp.dot(
                weights.astype(jnp.bfloat16), fresh_values, preferred_element_type=jnp.float32
            )
            rows = pl.ds(pl.multiple_of((4 + 2 * h + i) * 256, 256), 256)
            top[rows, :] = jnp.full((256, HD), LOW, jnp.float32)
            acc[rows, :] = jnp.zeros((256, 2 * HD), jnp.float32)
        return carried

    lax.fori_loop(0, 2, fresh_step, 0)
    forward(1)
    hand_out(1, 1)
    hand_out(5, 1)

    seen_key = jnp.broadcast_to(skv_ref[0:1, :HD].astype(jnp.float32), (PIECE, HD)).astype(
        jnp.bfloat16
    )

    def prepare(unit, place):
        for i, (p, ch) in enumerate(unit):
            for e in range(4):
                py, pc = peer(e)
                owner = py * 16 + plane_of(p) * 2 + pc
                for rank in range(2):
                    used = tabs_s[0, owner * 2 + rank] >= 0
                    cell = inbox[p, ch, e, pl.ds(rank * PIECE, PIECE), :]
                    rows = pl.ds(((i * 4 + e) * 2 + rank) * PIECE, PIECE)
                    keys[place, rows, :] = jnp.where(used, cell[:, :HD], seen_key)
                    values[place, rows, :HD] = jnp.where(
                        used, cell[:, HD:], jnp.zeros((PIECE, HD), jnp.bfloat16)
                    )
                    values[place, rows, HD:] = jnp.where(
                        used,
                        jnp.ones((PIECE, HD), jnp.bfloat16),
                        jnp.zeros((PIECE, HD), jnp.bfloat16),
                    )

    def whole(p):
        return [(p, ch) for ch in range(CHUNKS)]

    def tile_rows(tile):
        if isinstance(tile, int):
            return pl.ds(tile * TILE, TILE)
        return pl.ds(pl.multiple_of(tile * TILE, TILE), TILE)

    def score(place, tile, slot):
        scored[slot] = nt_dot(qall[tile_rows(tile), :], keys[place])

    def fold(place, tile, slot):
        rows = tile_rows(tile)
        parts = [scored[slot, :, j * HD : (j + 1) * HD] for j in range(4)]
        highest = top[rows, :]
        most = jnp.maximum(jnp.maximum(parts[0], parts[1]), jnp.maximum(parts[2], parts[3]))
        raised = jnp.maximum(
            highest, jnp.broadcast_to(jnp.max(most, axis=1, keepdims=True), (TILE, HD))
        )
        weights = jnp.concatenate(
            [jnp.exp2((part - raised) * SCALE).astype(jnp.bfloat16) for part in parts], axis=1
        )
        shrink = jnp.exp2((highest - raised) * SCALE)
        top[rows, :] = raised
        gained = jnp.dot(weights, values[place], preferred_element_type=jnp.float32)
        acc[rows, :HD] = acc[rows, :HD] * shrink + gained[:, :HD]
        acc[rows, HD:] = acc[rows, HD:] * shrink + gained[:, HD:]

    def attend(places):
        last = 4 * places - 1
        score(0, 0, 0)

        def two(j, carried):
            i = 2 * j
            score((i + 1) // 4, (i + 1) % 4, 1)
            fold(i // 4, i % 4, 0)
            after = jnp.minimum(i + 2, last)
            score(after // 4, after % 4, 0)
            fold((i + 1) // 4, (i + 1) % 4, 1)
            return carried

        lax.fori_loop(0, 2 * places, two, 0)

    both_chunks = tuple(range(CHUNKS))

    def collect(p, chunks):
        for ch in chunks:
            for e in range(1, 4):
                hand_copy(p, ch, e).wait_recv()

    for h in range(4):
        query_copy(h).wait_recv()
    collect(0, both_chunks)
    prepare(whole(0), 0)
    attend(1)

    for i in range(4):
        bundle_wait(i).wait_recv()
        moved = pltpu.make_async_copy(near.at[i], near_s.at[i], smem_sem.at[1 + i])
        moved.start()
        moved.wait()

    def near_copy(d, ch, e):
        return remote(
            near_stage.at[d, ch, e],
            inbox.at[(3, 7)[d], ch, e],
            nsend.at[d, ch, e],
            nrecv.at[d, ch, e],
            device(e, up_down[d]),
        )

    def far_copy(d, ch):
        return remote(
            wide_stage.at[ch, d],
            wide_in.at[ch, d],
            fsend.at[d, ch],
            frecv.at[d, ch],
            device(0, up_down[d]),
        )

    def last_copy(d, ch, e):
        place = inbox.at[4, ch, e]
        return remote(
            wide_in.at[ch, d, e],
            place,
            gsend.at[d, ch, e],
            grecv.at[d, ch, e],
            device(e, up_down[d]),
        )

    def on_way(d, hops):
        first = (z - hops * up_down[d] + NZ) % NZ
        return (first < 4) if d == 0 else (first >= 4)

    def if_used(d, ch, hops, do):
        pl.when(on_way(d, hops))(do)

    def send_far(ch):
        for d in range(2):
            ring(d, 2, ch).wait_recv()
            block = hop_bufs[d][1][ch]
            owner = yl * 16 + plane(-2 * up_down[d]) * 2 + c

            def send(d=d, block=block, owner=owner):
                for e in range(4):
                    for rank in range(2):
                        slot = asked(near_s.at[2 * d + 1], e, owner, rank)
                        wide_stage[ch, d, e, pl.ds(rank * PIECE, PIECE), :] = block[slot]
                far_copy(d, ch).start()

            if_used(d, ch, 2, send)

    def send_near(ch):
        for d in range(2):
            block = hop_bufs[d][1][ch]
            owner = yl * 16 + plane(-2 * up_down[d]) * 2 + c
            for e in (3, 2, 1, 0):
                for rank in range(2):
                    slot = asked(near_s.at[2 * d], e, owner, rank)
                    near_stage[d, ch, e, pl.ds(rank * PIECE, PIECE), :] = block[slot]
                near_copy(d, ch, e).start()

    def forward_far(ch):
        for d in range(2):

            def pass_on(d=d):
                far_copy(d, ch).wait_recv()
                for e in (3, 2, 1, 0):
                    last_copy(d, ch, e).start()

            if_used(d, ch, 3, pass_on)

    def pair_unit(p, ch, theirs=False):
        unit = [(p, ch), (p + 4, ch)]
        if p < 3:
            for q, _ in unit:
                collect(q, (ch,))
        else:
            for d in range(2):
                for e in range(4):
                    near_copy(d, ch, e).wait_recv()
        prepare(unit, 0)
        if theirs:
            score(0, 2, 0)
            score(0, 3, 1)
            fold(0, 2, 0)
            fold(0, 3, 1)
        else:
            attend(1)

    pair_unit(1, 0)
    send_far(0)
    send_near(0)
    hand_out(2, 0)
    hand_out(6, 0)
    send_far(1)
    send_near(1)
    hand_out(2, 1)
    hand_out(6, 1)
    pair_unit(1, 1)
    forward_far(0)
    pair_unit(2, 0)
    forward_far(1)
    pair_unit(2, 1)
    pair_unit(3, 0)
    pair_unit(3, 1, True)
    for d, ch in both:

        def arrive(d=d, ch=ch):
            for e in range(4):
                last_copy(d, ch, e).wait_recv()

        if_used(d, ch, 4, arrive)
    prepare(whole(4), 1)

    def part_copy(i):
        return remote(part_out.at[i], part_in.at[i], osend.at[i], orecv.at[i], xid)

    def stat_copy():
        return remote(stat_out, stat_in, ssend.at[0], srecv.at[0], xid)

    def send_part(i):
        part_out[i] = acc[pl.ds((2 + i) * TILE, TILE), :HD].astype(jnp.bfloat16)
        part_copy(i).start()

    def send_stats():
        for i in range(2):
            for j in range(4):
                rows = pl.ds((2 + i) * TILE + j * HD, HD)
                stat_out[i, j : j + 1, :] = as_row(top[rows, :])
                stat_out[i, 4 + j : 5 + j, :] = as_row(acc[rows, HD:])
        stat_copy().start()

    score(1, 2, 0)
    score(1, 3, 1)
    fold(1, 2, 0)
    send_part(0)
    score(0, 0, 0)
    fold(1, 3, 1)
    send_stats()
    send_part(1)
    score(0, 1, 1)
    fold(0, 0, 0)
    score(1, 0, 0)
    fold(0, 1, 1)
    score(1, 1, 1)
    fold(1, 0, 0)
    fold(1, 1, 1)

    for d, ch in both:
        ring(d, 1, ch).wait_send()
        ring(d, 2, ch).wait_send()
        for e in range(4):
            near_copy(d, ch, e).wait_send()

        def sent(d=d, ch=ch):
            far_copy(d, ch).wait_send()

        def passed(d=d, ch=ch):
            for e in range(4):
                last_copy(d, ch, e).wait_send()

        if_used(d, ch, 2, sent)
        if_used(d, ch, 3, passed)
    for i in range(4):
        bundle_copy(i).wait_send()
        query_copy(i).wait_send()
    for e in range(1, 4):
        table_copy(e).wait_send()
        for p in (0, 1, 2, 5, 6):
            for ch in range(CHUNKS):
                hand_copy(p, ch, e).wait_send()
    stored = [decoded]
    stat_copy().wait_recv()
    for i in range(2):
        for j in range(4):
            rows = pl.ds(i * TILE + j * HD, HD)
            here = top[rows, :]
            there = jnp.broadcast_to(column(stat_in[i, j : j + 1, :]), (HD, HD))
            extra = jnp.broadcast_to(column(stat_in[i, 4 + j : 5 + j, :]), (HD, HD))
            peak = jnp.maximum(here, there)
            keep, take = jnp.exp2((here - peak) * SCALE), jnp.exp2((there - peak) * SCALE)
            inverse = 1.0 / (acc[rows, HD:] * keep + extra * take)
            acc[rows, :HD] = acc[rows, :HD] * (keep * inverse)
            top[rows, :] = take * inverse
    for h in range(4):
        if h % 2 == 0:
            part_copy(h // 2).wait_recv()
        rows = pl.ds(h * 256, 256)
        other = part_in[h // 2, pl.ds(h % 2 * 256, 256), :].astype(jnp.float32)
        span_out[:, pl.ds(h * HD, HD)] = (acc[rows, :HD] + other * top[rows, :]).astype(
            jnp.bfloat16
        )
        stored.append(
            pltpu.make_async_copy(
                span_out.at[:, pl.ds(h * HD, HD)],
                span_hbm.at[:, pl.ds(h * HD, HD)],
                store_sem.at[1 + h],
            )
        )
        stored[-1].start()

    for i in range(2):
        part_copy(i).wait_send()
    stat_copy().wait_send()
    for copy in stored:
        copy.wait()


def staged(*refs):
    first = 9 + 2 + 9 + 2
    flat = refs[first : first + 8]
    bufs = tuple(tuple(tuple(flat[(d * 2 + k) * 2 + ch] for ch in range(2)) for k in range(2)) for d in range(2))
    kernel(*refs[:first], bufs, *refs[first + 8 :])


def place_results(span_ref, decode_ref, span_out, decode_out):
    span_out[...] = span_ref[...]
    decode_out[...] = decode_ref[...]


def local(
    span_query,
    span_kv,
    kv_pool,
    hit_owner,
    hit_slot,
    decode_query,
    decode_kv,
    decode_table,
    decode_length,
):
    hbm = pl.BlockSpec(memory_space=pl.ANY)
    dma = pltpu.SemaphoreType.DMA
    bf16, f32 = jnp.bfloat16, jnp.float32
    results = pl.pallas_call(
        staged,
        out_shape=(
            jax.ShapeDtypeStruct(span_query.shape, bf16),
            jax.ShapeDtypeStruct(decode_query.shape, bf16),
        ),
        in_specs=[hbm] * 9,
        out_specs=(hbm, hbm),
        scratch_shapes=[
            pltpu.SMEM((32,), jnp.int32),
            pltpu.SMEM((32,), jnp.int32),
            pltpu.VMEM((4, 32), jnp.int32),
            pltpu.VMEM((1, 32), jnp.int32),
            pltpu.VMEM(decode_query.shape, bf16),
            pltpu.VMEM(decode_kv.shape, bf16),
            pltpu.VMEM(span_kv.shape, bf16),
            pltpu.VMEM(span_query.shape, bf16),
            pltpu.VMEM(decode_query.shape, bf16),
            pltpu.VMEM((16, 128, 256), bf16),
            pltpu.VMEM((2048, HD), bf16),
        ]
        + [pltpu.VMEM((16, PIECE, 256), bf16)] * 8
        + [
            pltpu.VMEM((5, CHUNKS, 4, 2 * PIECE, 256), bf16),
            pltpu.VMEM((2, CHUNKS, 4, 2 * PIECE, 256), bf16),
            pltpu.VMEM((2, 2, 4, 2 * PIECE, 256), bf16),
            pltpu.VMEM((2, 2, 4, 2 * PIECE, 256), bf16),
            pltpu.VMEM((NZ, CHUNKS, 4, 2 * PIECE, 256), bf16),
            pltpu.VMEM((4, 8, 128), jnp.int32),
            pltpu.SMEM((8, 128), jnp.int32),
            pltpu.VMEM((8, 128), jnp.int32),
            pltpu.VMEM((4, 8, 128), jnp.int32),
            pltpu.SMEM((4, 8, 128), jnp.int32),
            pltpu.VMEM((2, 512, HD), bf16),
            pltpu.VMEM((2, 512, 2 * HD), bf16),
            pltpu.VMEM((2, TILE, 512), f32),
            pltpu.VMEM((2048, 2 * HD), f32),
            pltpu.VMEM((2048, HD), f32),
            pltpu.VMEM((2, TILE, HD), bf16),
            pltpu.VMEM((2, TILE, HD), bf16),
            pltpu.VMEM((2, 8, 128), f32),
            pltpu.VMEM((2, 8, 128), f32),
            dma((12,)),
            dma((5,)),
            dma((2, 2, CHUNKS)),
            dma((2, 2, CHUNKS)),
            dma((NZ, CHUNKS, 4)),
            dma((NZ, CHUNKS, 4)),
            dma((2, CHUNKS, 4)),
            dma((2, CHUNKS, 4)),
            dma((2, CHUNKS)),
            dma((2, CHUNKS)),
            dma((2, CHUNKS, 4)),
            dma((2, CHUNKS, 4)),
            dma((4,)),
            dma((4,)),
            dma((4,)),
            dma((4,)),
            dma((5,)),
            dma((4,)),
            dma((4,)),
            dma((2,)),
            dma((2,)),
            dma((1,)),
            dma((1,)),
        ],
        compiler_params=pltpu.CompilerParams(
            collective_id=0, has_side_effects=True, vmem_limit_bytes=56 * 1024 * 1024
        ),
        cost_estimate=pl.CostEstimate(
            flops=5 * 10**9, bytes_accessed=3 * 2**20, transcendentals=10**7
        ),
        name="spanned_attention",
    )(
        hit_owner.reshape(-1),
        hit_slot,
        decode_table.T,
        decode_length,
        decode_query,
        decode_kv,
        span_kv,
        span_query,
        kv_pool,
    )
    vmem = pl.BlockSpec(memory_space=pltpu.VMEM)
    return pl.pallas_call(
        place_results,
        out_shape=(
            jax.ShapeDtypeStruct(span_query.shape, bf16),
            jax.ShapeDtypeStruct(decode_query.shape, bf16),
        ),
        in_specs=[vmem] * 2,
        out_specs=(vmem,) * 2,
        name="place_results",
    )(*results)


def solution(mesh):
    placed = (
        P("replica", "tensor"),
        P("replica", "tensor"),
        P("replica", None, "tensor"),
        P("replica", None),
        P("replica"),
        P("replica", "tensor"),
        P("replica", "tensor"),
        P("replica", None),
        P("replica", None),
    )
    return jax.shard_map(
        local,
        mesh=mesh,
        in_specs=placed,
        out_specs=(P("replica", "tensor"), P("replica", "tensor")),
        check_vma=False,
    )
```
